256 devices in a mesh: dp: 4 (over y), context: 16 (over z, core), tensor: 4 (over x).
Axes of the slice: x: 4, y: 4, z: 8, core: 2. Of those that a mesh axis runs over, the one named last changes fastest.
Arguments:
- cross_query: bfloat16 [4, 4096, 8192], P('dp', 'context', 'tensor'), may hold values from -28 to 28
- cross_grad: bfloat16 [4, 4096, 8192], P('dp', 'context', 'tensor'), may hold values from -48 to 48
- neighbour_kv: bfloat16 [512, 128, 2, 1024], P(('dp', 'context', 'tensor')), may hold values from -6 to 6
- span_neighbours: int32 [4, 64, 2], replicated, may hold values from 0 to 511, as said below
Outputs:
- cross_out: bfloat16 [4, 4096, 8192], P('dp', 'context', 'tensor')
- neighbour_grad: bfloat16 [512, 128, 2, 1024], P(('dp', 'context', 'tensor'))
The draws below stay inside these ranges and needn't reach their ends.
Inputs may be any that keep to these rules, and one draw needn't show every extreme that they name: `span_neighbours`: every row of neighbour_kv is listed exactly once. Span u of sequence b lists only rows stored on devices (of any dp and tensor index) whose context index is that of the positions of span u; such a row's owner is b. Both rows of one device have the same owner; which owner that is differs between devices.
All inputs are finite; a program needn't handle non-finite values.
Results may differ from the reference program's by a relative error of at most 0.005.
Values may be sent and summed in bfloat16 or wider, within the bound.
No kernel may reach another device: no remote copies, remote signals or barrier semaphores. Data moves between devices by JAX's collectives and lax.ppermute only.
A program may use at most 64 MiB of HBM per device.

```python
import math
import jax
import jax.numpy as jnp
from jax import lax

HEADS = 64
KV_HEADS = 8
HD = 128
SPAN = 64
NL = 128
KNB = 2
G = 8
SEQS = 4
SEQ = 4096
SPANS_ALL = 64
NB_E = 2
CAP = 2
NBS = 512
N_DP = 4
N_CONTEXT = 16
N_TENSOR = 4


def routing(key):
    keyed = jax.random.fold_in(key, 101)
    columns = N_CONTEXT * N_TENSOR
    split_keys = jax.random.split(keyed, columns + 1)
    shuffles = jax.vmap(lambda member: jax.random.permutation(member, N_DP))(split_keys[:columns])
    row_index = jnp.arange(NB_E)
    others = max(N_DP - 1, 1)
    pattern = jnp.where(row_index < CAP, 0, 1 + (row_index - CAP) % others)
    shifts = shuffles[:, pattern]
    source_dp = jnp.arange(N_DP)
    owners = ((source_dp[:, None, None] + shifts[None]) % N_DP).reshape(-1)
    global_row = jnp.arange(NBS)
    column_context = global_row // (N_TENSOR * NB_E) % N_CONTEXT
    shuffle_rank = jax.random.permutation(split_keys[columns], NBS)
    sorted_rows = jnp.argsort((owners * N_CONTEXT + column_context) * NBS + shuffle_rank)
    return sorted_rows.reshape(SEQS, SPANS_ALL, KNB).astype(jnp.int32)


def draw_span_neighbours(key, part):
    return routing(key)


def draw_cross_query(key, part):
    keyed = jax.random.fold_in(key, 5)
    array_shape = (SEQS, SEQ, KV_HEADS, G, HD)
    drawn = jax.random.truncated_normal(keyed, -6.0, 6.0, array_shape, jnp.float32)
    return drawn.reshape(SEQS, SEQ, HEADS * HD).astype(jnp.bfloat16)


def draw_neighbour_kv(key, part):
    keyed = jax.random.fold_in(key, 9)
    array_shape = (NBS, NL, 2, KV_HEADS, HD)
    drawn = jax.random.truncated_normal(keyed, -6.0, 6.0, array_shape, jnp.float32)
    return drawn.reshape(NBS, NL, 2, KV_HEADS * HD).astype(jnp.bfloat16)


def shard_levels(own_key, shape, pieces, least, top_value):
    gain, own = 1.0, jax.random.fold_in(own_key, 6)
    for dim, parts in pieces:
        heights = jnp.exp(jax.random.uniform(jax.random.fold_in(own, dim), (parts,), jnp.float32, least / len(pieces), top_value / len(pieces)))
        gain = gain * jnp.repeat(heights, shape[dim] // parts).reshape([-1 if axis == dim else 1 for axis in range(len(shape))])
    return gain


def gaussian(rng, extent, deviation, bound, cuts=(), held_as=jnp.bfloat16):
    values = deviation * jax.random.normal(rng, extent, jnp.float32)
    if cuts:
        values = values * shard_levels(rng, extent, cuts, -0.22, 0.18)
    return jnp.clip(values, -bound, bound).astype(held_as)


def setup_inputs(seed: int = 0) -> dict:
    seeds = jax.random.split(jax.random.key(seed), 5)
    cross_query = draw_cross_query(jax.random.fold_in(seeds[4], 71), 0)
    cross_grad = gaussian(seeds[1], (SEQS, SEQ, HEADS * HD), 8.0, 48.0, ((0, 4), (1, 16), (2, 4)))
    neighbour_kv = draw_neighbour_kv(jax.random.fold_in(seeds[4], 71), 0)
    span_neighbours = draw_span_neighbours(jax.random.fold_in(seeds[4], 71), 0)
    return dict(cross_query=cross_query, cross_grad=cross_grad, neighbour_kv=neighbour_kv, span_neighbours=span_neighbours)


def rounded(values):
    return lax.optimization_barrier(values.astype(jnp.bfloat16)).astype(jnp.float32)

def cross_sequence(queries, cotangent, selected):
    score_scale = 1.0 / math.sqrt(HD)
    query_width = HEADS * HD
    windows = SPANS_ALL + 1

    def extend(values):
        head_rows = jnp.zeros((1, query_width), values.dtype)
        tail_rows = jnp.zeros((SPAN - 1, query_width), values.dtype)
        joined = jnp.concatenate([head_rows, values, tail_rows], 0)
        return joined.reshape(windows, SPAN, KV_HEADS, G, HD).astype(jnp.float32)
    query_five = extend(queries)
    grad_five = extend(cotangent)
    empty_rows = jnp.zeros((1,) + selected.shape[1:], selected.dtype)
    context_rows = jnp.concatenate([empty_rows, selected], 0)
    context_rows = context_rows.reshape(windows, KNB * NL, 2, KV_HEADS, HD).astype(jnp.float32)
    key_part = context_rows[:, :, 0]
    value_part = context_rows[:, :, 1]
    scores = jnp.einsum('wqkgd,wnkd->wkgqn', query_five, key_part) * score_scale
    peak_value = lax.optimization_barrier(jnp.max(scores, axis=-1, keepdims=True))
    raised = jnp.exp(scores - peak_value)
    weights = raised / lax.optimization_barrier(jnp.sum(raised, axis=-1, keepdims=True))
    weights_low = rounded(weights)
    output = jnp.einsum('wkgqn,wnkd->wqkgd', weights_low, value_part)
    output = output.reshape(windows * SPAN, query_width)[1:SEQ + 1]
    weight_slope = jnp.einsum('wqkgd,wnkd->wkgqn', grad_five, value_part)
    centre = lax.optimization_barrier(jnp.sum(weights * weight_slope, axis=-1, keepdims=True))
    score_grad = rounded(weights * (weight_slope - centre) * score_scale)
    key_grad = jnp.einsum('wkgqn,wqkgd->wnkd', score_grad, query_five)
    value_grad = jnp.einsum('wkgqn,wqkgd->wnkd', weights_low, grad_five)
    stacked = jnp.stack([key_grad, value_grad], 2)[1:]
    return (output, stacked.reshape(SPANS_ALL * KNB, NL, 2, KV_HEADS * HD))

def reference(cross_query, cross_grad, neighbour_kv, span_neighbours):

    def cross_one(members):
        queries, cotangent, listed = members
        selected = neighbour_kv[listed.reshape(-1)]
        selected = selected.reshape(SPANS_ALL, KNB * NL, 2, KV_HEADS * HD)
        return cross_sequence(queries, cotangent, selected)
    outputs, gradients = lax.map(cross_one, (cross_query, cross_grad, span_neighbours))
    cross_out = outputs.astype(jnp.bfloat16)
    flat_ids = span_neighbours.reshape(-1).astype(jnp.int32)
    neighbour_grad = jnp.zeros(neighbour_kv.shape, jnp.float32).at[flat_ids].set(gradients.reshape(-1, NL, 2, KV_HEADS * HD))
    return (cross_out, neighbour_grad.astype(jnp.bfloat16))
```

```python
import functools
import math

import jax
import jax.numpy as jnp
from jax import lax
from jax.experimental import pallas as pl
from jax.experimental.pallas import tpu as pltpu
from jax.sharding import PartitionSpec as P

HD = 128
SPAN = 64
NL = 128
KNB = 2
SLOTS = 2
LOG2E = 1.4426950408889634


def nt(a, b):
    return lax.dot_general(a, b, (((1,), (1,)), ((), ())), preferred_element_type=jnp.float32)


def nn(a, b):
    return lax.dot_general(a, b, (((1,), (0,)), ((), ())), preferred_element_type=jnp.float32)


def source_of(row, geometry):
    local_rows, context_size, tensor_size = geometry
    device = row // local_rows
    return device // (context_size * tensor_size) * tensor_size + device % tensor_size


def sources_of_owner(ids_ref, owner, count, per_owner, geometry):
    local_rows = geometry[0]
    found = [jnp.int32(0)] * per_owner
    seen = jnp.int32(0)
    for k in range(count):
        row = ids_ref[owner * count + k]
        first = row % local_rows == 0
        source = source_of(row, geometry)
        for m in range(per_owner):
            found[m] = jnp.where(first & (seen == m), source, found[m])
        seen = seen + first.astype(jnp.int32)
    return found


def deliver_kernel(ids_ref, held_ref, out_ref, *, owners, count, geometry):
    tensor_size = geometry[2]
    per_owner = out_ref.shape[1]
    width = out_ref.shape[3]
    for owner in range(owners):
        sources = sources_of_owner(ids_ref, owner, count, per_owner, geometry)
        for m in range(per_owner):
            block = held_ref[sources[m]]
            for t in range(tensor_size):
                out_ref[owner * tensor_size + t, m] = block[:, t * width : (t + 1) * width]


def collect_kernel(ids_ref, held_ref, out_ref, *, owners, count, geometry):
    tensor_size = geometry[2]
    per_owner = held_ref.shape[1]
    width = held_ref.shape[3]
    for owner in range(owners):
        sources = sources_of_owner(ids_ref, owner, count, per_owner, geometry)
        for m in range(per_owner):
            for t in range(tensor_size):
                out_ref[sources[m], :, t * width : (t + 1) * width] = held_ref[
                    owner * tensor_size + t, m
                ]


def attention_kernel(ids_ref, q_ref, g_ref, kv_ref, out_ref, grad_ref, *, count, geometry):
    local_rows = geometry[0]
    rows = kv_ref.shape[2]
    pieces = NL // rows
    kv_heads = kv_ref.shape[3] // HD
    groups = q_ref.shape[1] // (kv_heads * HD)
    scale = 1.0 / math.sqrt(HD)
    window = pl.program_id(0)
    places = []
    for n in range(KNB):
        row = ids_ref[window * KNB + n]
        start = row // local_rows * local_rows
        part = row % local_rows
        seen = jnp.int32(0)
        rank = jnp.int32(0)
        for k in range(count):
            other = ids_ref[k]
            rank = jnp.where(other == start, seen, rank)
            seen = seen + (other % local_rows == 0).astype(jnp.int32)
        for i in range(pieces):
            places.append((part * pieces + i, rank))
    half = local_rows * pieces
    for h in range(kv_heads):
        lanes = slice(h * HD, (h + 1) * HD)
        key = jnp.concatenate([kv_ref[j, m, :, lanes] for j, m in places], 0)
        value = jnp.concatenate([kv_ref[half + j, m, :, lanes] for j, m in places], 0)
        heads = [slice((h * groups + g) * HD, (h * groups + g + 1) * HD) for g in range(groups)]
        query = jnp.concatenate([q_ref[:, s] for s in heads], 0)
        grad = jnp.concatenate([g_ref[:, s] for s in heads], 0)
        scores = nt(key, query) * (scale * LOG2E)
        raised = jnp.exp2(scores - jnp.max(scores, axis=0, keepdims=True))
        weights = raised * (1.0 / jnp.sum(raised, axis=0, keepdims=True))
        low = weights.astype(jnp.bfloat16)
        out = nn(value.T, low).T.astype(jnp.bfloat16)
        for g, s in enumerate(heads):
            out_ref[:, s] = out[g * SPAN : (g + 1) * SPAN]
        value_grad = nn(low, grad).astype(jnp.bfloat16)
        slope = nt(value, grad)
        centre = jnp.sum(weights * slope, axis=0, keepdims=True)
        score_grad = (weights * (slope - centre) * scale).astype(jnp.bfloat16)
        key_grad = nn(score_grad, query).astype(jnp.bfloat16)
        for b, (j, m) in enumerate(places):
            grad_ref[j, m, :, lanes] = key_grad[b * rows : (b + 1) * rows]
            grad_ref[half + j, m, :, lanes] = value_grad[b * rows : (b + 1) * rows]


def whole(shape):
    return pl.BlockSpec(shape, lambda *_: (0,) * len(shape))


def shards(cross_query, cross_grad, neighbour_kv, span_neighbours):
    dp_size = lax.axis_size("dp")
    context_size = lax.axis_size("context")
    tensor_size = lax.axis_size("tensor")
    local_rows, _, _, kv_width = neighbour_kv.shape
    width = kv_width // tensor_size
    row_count, query_width = cross_query.shape[1:]
    spans = row_count // SPAN
    count = spans * KNB
    peers = dp_size * tensor_size
    per_owner = count // local_rows
    rows = local_rows * NL * SLOTS // peers
    pieces = NL // rows
    geometry = (local_rows, context_size, tensor_size)
    group = ("dp", "tensor")
    params = pltpu.CompilerParams(vmem_limit_bytes=32 * 1024 * 1024)

    back = [(i + 1, i) for i in range(context_size - 1)]
    forth = [(i, i + 1) for i in range(context_size - 1)]
    query = cross_query[0]
    grad = cross_grad[0]
    next_query = lax.ppermute(query[:SPAN], "context", back)
    next_grad = lax.ppermute(grad[:SPAN], "context", back)

    def ahead(own, following):
        return jnp.concatenate([own[SPAN - 1 :], following[: SPAN - 1]], 0)

    ids = lax.dynamic_slice_in_dim(
        span_neighbours, lax.axis_index("context") * spans, spans, 1
    ).reshape(-1)
    own_ids = lax.dynamic_slice_in_dim(ids, lax.axis_index("dp") * count, count, 0)

    spread = neighbour_kv.reshape(local_rows, pieces, rows, SLOTS, kv_width)
    spread = spread.transpose(3, 0, 1, 2, 4).reshape(peers, rows, kv_width)
    held = lax.all_to_all(spread, group, 0, 0, tiled=True)
    smem = pl.BlockSpec(memory_space=pltpu.SMEM)
    vmem = pl.BlockSpec(memory_space=pltpu.VMEM)
    delivered = pl.pallas_call(
        functools.partial(deliver_kernel, owners=dp_size, count=count, geometry=geometry),
        out_shape=jax.ShapeDtypeStruct((peers, per_owner, rows, width), jnp.bfloat16),
        in_specs=[smem, vmem],
        out_specs=vmem,
        compiler_params=params,
        name="deliver",
    )(ids, held)
    kv = lax.all_to_all(delivered, group, 0, 0, tiled=True)
    block = pl.BlockSpec((SPAN, query_width), lambda w: (w, 0))
    out_rows, kv_grad = pl.pallas_call(
        functools.partial(attention_kernel, count=count, geometry=geometry),
        grid=(spans,),
        out_shape=(
            jax.ShapeDtypeStruct((row_count, query_width), jnp.bfloat16),
            jax.ShapeDtypeStruct(kv.shape, jnp.bfloat16),
        ),
        in_specs=[smem, block, block, whole(kv.shape)],
        out_specs=(block, whole(kv.shape)),
        compiler_params=params,
        name="attention",
    )(own_ids, ahead(query, next_query), ahead(grad, next_grad), kv)
    before = lax.ppermute(out_rows[row_count - SPAN :], "context", forth)
    cross_out = jnp.concatenate([before[1:], out_rows[: row_count - SPAN + 1]], 0)

    returned = lax.all_to_all(kv_grad, group, 0, 0, tiled=True)
    collected = pl.pallas_call(
        functools.partial(collect_kernel, owners=dp_size, count=count, geometry=geometry),
        out_shape=jax.ShapeDtypeStruct((peers, rows, kv_width), jnp.bfloat16),
        in_specs=[smem, vmem],
        out_specs=vmem,
        compiler_params=params,
        name="collect",
    )(ids, returned)
    final = lax.all_to_all(collected, group, 0, 0, tiled=True)
    final = final.reshape(SLOTS, local_rows, pieces, rows, kv_width).transpose(1, 2, 3, 0, 4)
    return (cross_out[None], final.reshape(neighbour_kv.shape))


def solution(mesh):
    return jax.shard_map(
        shards,
        mesh=mesh,
        in_specs=(
            P("dp", "context", "tensor"),
            P("dp", "context", "tensor"),
            P(("dp", "context", "tensor"), None, None, None),
            P(),
        ),
        out_specs=(P("dp", "context", "tensor"), P(("dp", "context", "tensor"), None, None, None)),
        check_vma=False,
    )
```

```python
import functools
import math

import jax
import jax.numpy as jnp
from jax import lax
from jax.experimental import pallas as pl
from jax.experimental.pallas import tpu as pltpu
from jax.sharding import PartitionSpec as P

HD = 128
SPAN = 64
NL = 128
KNB = 2
SLOTS = 2
LOG2E = 1.4426950408889634


def nt(a, b):
    return lax.dot_general(a, b, (((1,), (1,)), ((), ())), preferred_element_type=jnp.float32)


def nn(a, b):
    return lax.dot_general(a, b, (((1,), (0,)), ((), ())), preferred_element_type=jnp.float32)


def place_of(row, geometry):
    local_rows, context_size, tensor_size = geometry
    device = row // local_rows
    source = device // (context_size * tensor_size) * tensor_size + device % tensor_size
    return source, row % local_rows


def deliver_kernel(ids_ref, held_ref, *out_refs, geometry):
    owners = len(out_refs)
    count = out_refs[0].shape[0]
    me = ids_ref[owners * count]
    for s, out_ref in enumerate(out_refs):
        owner = (me + s) % owners
        for k in range(count):
            source, part = place_of(ids_ref[owner * count + k], geometry)
            for slot in range(SLOTS):
                out_ref[k, slot] = held_ref[source, slot, part]


def collect_kernel(ids_ref, *refs, geometry):
    held_refs, out_ref = refs[:-1], refs[-1]
    owners = len(held_refs)
    count = held_refs[0].shape[0]
    me = ids_ref[owners * count]
    for s, held_ref in enumerate(held_refs):
        owner = (me + s) % owners
        for k in range(count):
            source, part = place_of(ids_ref[owner * count + k], geometry)
            for slot in range(SLOTS):
                out_ref[source, slot, part] = held_ref[k, slot]


def attention_kernel(q_ref, g_ref, *refs):
    parts = len(refs) // 2
    kv_refs, out_ref, grad_refs = refs[:parts], refs[parts], refs[parts + 1 :]
    rows = kv_refs[0].shape[2]
    kv_heads = kv_refs[0].shape[3] // HD
    groups = q_ref.shape[1] // (kv_heads * HD)
    scale = 1.0 / math.sqrt(HD)
    places = [(p, n) for p in range(parts) for n in range(KNB)]
    for h in range(kv_heads):
        lanes = slice(h * HD, (h + 1) * HD)
        key = jnp.concatenate([kv_refs[p][n, 0, :, lanes] for p, n in places], 0)
        value = jnp.concatenate([kv_refs[p][n, 1, :, lanes] for p, n in places], 0)
        heads = [slice((h * groups + g) * HD, (h * groups + g + 1) * HD) for g in range(groups)]
        query = jnp.concatenate([q_ref[:, s] for s in heads], 0)
        grad = jnp.concatenate([g_ref[:, s] for s in heads], 0)
        scores = nt(key, query) * (scale * LOG2E)
        raised = jnp.exp2(scores - jnp.max(scores, axis=0, keepdims=True))
        weights = raised * (1.0 / jnp.sum(raised, axis=0, keepdims=True))
        low = weights.astype(jnp.bfloat16)
        out = nn(value.T, low).T.astype(jnp.bfloat16)
        for g, s in enumerate(heads):
            out_ref[:, s] = out[g * SPAN : (g + 1) * SPAN]
        value_grad = nn(low, grad).astype(jnp.bfloat16)
        slope = nt(value, grad)
        centre = jnp.sum(weights * slope, axis=0, keepdims=True)
        score_grad = (weights * (slope - centre) * scale).astype(jnp.bfloat16)
        key_grad = nn(score_grad, query).astype(jnp.bfloat16)
        for b, (p, n) in enumerate(places):
            grad_refs[p][n, 0, :, lanes] = key_grad[b * rows : (b + 1) * rows]
            grad_refs[p][n, 1, :, lanes] = value_grad[b * rows : (b + 1) * rows]


def shards(cross_query, cross_grad, neighbour_kv, span_neighbours):
    dp_size = lax.axis_size("dp")
    context_size = lax.axis_size("context")
    tensor_size = lax.axis_size("tensor")
    local_rows, _, _, kv_width = neighbour_kv.shape
    width = kv_width // tensor_size
    row_count, query_width = cross_query.shape[1:]
    spans = row_count // SPAN
    count = spans * KNB
    peers = dp_size * tensor_size
    rows = NL // dp_size
    geometry = (local_rows, context_size, tensor_size)
    group = ("dp", "tensor")
    params = pltpu.CompilerParams(vmem_limit_bytes=32 * 1024 * 1024)
    smem = pl.BlockSpec(memory_space=pltpu.SMEM)
    vmem = pl.BlockSpec(memory_space=pltpu.VMEM)

    def ring(array, by):
        return lax.ppermute(array, "dp", [(i, (i + by) % dp_size) for i in range(dp_size)])

    spread = neighbour_kv.transpose(2, 0, 1, 3)
    spread = spread.reshape(SLOTS, local_rows, dp_size, rows, tensor_size, width)
    spread = spread.transpose(2, 4, 0, 1, 3, 5).reshape(peers, SLOTS, local_rows, rows, width)
    held = lax.all_to_all(spread, group, 0, 0, tiled=True)

    ids = lax.dynamic_slice_in_dim(
        span_neighbours, lax.axis_index("context") * spans, spans, 1
    ).reshape(-1)
    ids = jnp.concatenate([ids, lax.axis_index("dp").astype(jnp.int32)[None]])

    held, halo_query, halo_grad = lax.optimization_barrier(
        (held, cross_query[0, :SPAN], cross_grad[0, :SPAN])
    )
    back = [(i + 1, i) for i in range(context_size - 1)]
    forth = [(i, i + 1) for i in range(context_size - 1)]
    following = lax.ppermute(jnp.stack([halo_query, halo_grad]), "context", back)
    query = jnp.concatenate([cross_query[0, SPAN - 1 :], following[0, : SPAN - 1]], 0)
    grad = jnp.concatenate([cross_grad[0, SPAN - 1 :], following[1, : SPAN - 1]], 0)

    part = jax.ShapeDtypeStruct((count, SLOTS, rows, width), jnp.bfloat16)
    delivered = pl.pallas_call(
        functools.partial(deliver_kernel, geometry=geometry),
        out_shape=(part,) * dp_size,
        in_specs=[smem, vmem],
        out_specs=(vmem,) * dp_size,
        compiler_params=params,
        name="deliver",
    )(ids, held)
    order = sorted(range(1, dp_size), key=lambda s: -min(s, dp_size - s))
    kv = {0: delivered[0]}
    for s in order:
        kv[s] = ring(delivered[s], s)
    block = pl.BlockSpec((SPAN, query_width), lambda w: (w, 0))
    kv_block = pl.BlockSpec((KNB, SLOTS, rows, width), lambda w: (w, 0, 0, 0))
    out_rows, *kv_grads = pl.pallas_call(
        attention_kernel,
        grid=(spans,),
        out_shape=(jax.ShapeDtypeStruct((row_count, query_width), jnp.bfloat16),)
        + (part,) * dp_size,
        in_specs=[block, block] + [kv_block] * dp_size,
        out_specs=(block,) + (kv_block,) * dp_size,
        compiler_params=params,
        name="attention",
    )(query, grad, *[kv[s] for s in range(dp_size)])
    returned = {0: kv_grads[0]}
    for s in order:
        returned[s] = ring(kv_grads[s], -s)

    before = lax.ppermute(out_rows[row_count - SPAN :], "context", forth)
    cross_out = jnp.concatenate([before[1:], out_rows[: row_count - SPAN + 1]], 0)

    collected = pl.pallas_call(
        functools.partial(collect_kernel, geometry=geometry),
        out_shape=jax.ShapeDtypeStruct(held.shape, jnp.bfloat16),
        in_specs=[smem] + [vmem] * dp_size,
        out_specs=vmem,
        compiler_params=params,
        name="collect",
    )(ids, *[returned[s] for s in range(dp_size)])
    final = lax.all_to_all(collected, group, 0, 0, tiled=True)
    final = final.reshape(dp_size, tensor_size, SLOTS, local_rows, rows, width)
    final = final.transpose(3, 0, 4, 2, 1, 5)
    return (cross_out[None], final.reshape(neighbour_kv.shape))


def solution(mesh):
    return jax.shard_map(
        shards,
        mesh=mesh,
        in_specs=(
            P("dp", "context", "tensor"),
            P("dp", "context", "tensor"),
            P(("dp", "context", "tensor"), None, None, None),
            P(),
        ),
        out_specs=(P("dp", "context", "tensor"), P(("dp", "context", "tensor"), None, None, None)),
        check_vma=False,
    )
```

```python
import functools
import math

import jax
import jax.numpy as jnp
from jax import lax
from jax.experimental import pallas as pl
from jax.experimental.pallas import tpu as pltpu
from jax.sharding import PartitionSpec as P

HD = 128
SPAN = 64
NL = 128
KNB = 2
SLOTS = 2
CHUNKS = 2
LOG2E = 1.4426950408889634


def nt(a, b):
    return lax.dot_general(a, b, (((1,), (1,)), ((), ())), preferred_element_type=jnp.float32)


def nn(a, b):
    return lax.dot_general(a, b, (((1,), (0,)), ((), ())), preferred_element_type=jnp.float32)


def place_of(row, geometry):
    local_rows, context_size, tensor_size = geometry
    device = row // local_rows
    source = device // (context_size * tensor_size) * tensor_size + device % tensor_size
    return source, row % local_rows


def deliver_kernel(ids_ref, held_ref, *out_refs, owners, geometry):
    length = out_refs[0].shape[0]
    count = len(out_refs) // owners * length
    me = ids_ref[owners * count]
    for o, out_ref in enumerate(out_refs):
        owner = (me + o % owners) % owners
        for k in range(length):
            row = ids_ref[owner * count + o // owners * length + k]
            source, part = place_of(row, geometry)
            for slot in range(SLOTS):
                out_ref[k, slot] = held_ref[source, slot, part]


def collect_kernel(ids_ref, *refs, owners, geometry):
    held_refs, out_ref = refs[:-1], refs[-1]
    length = held_refs[0].shape[0]
    count = len(held_refs) // owners * length
    me = ids_ref[owners * count]
    for o, held_ref in enumerate(held_refs):
        owner = (me + o % owners) % owners
        for k in range(length):
            row = ids_ref[owner * count + o // owners * length + k]
            source, part = place_of(row, geometry)
            for slot in range(SLOTS):
                out_ref[source, slot, part] = held_ref[k, slot]


def attention_kernel(*refs, parts, halo):
    ahead_refs, refs = refs[:2], refs[2:]
    last_refs, refs = refs[:2], refs[2:]
    if halo:
        halo_refs, refs = refs[:2], refs[2:]
        at_end = pl.program_id(0) == pl.num_programs(0) - 1
    kv_refs, out_ref, grad_refs = refs[:parts], refs[parts], refs[parts + 1 :]
    rows = kv_refs[0].shape[2]
    kv_heads = kv_refs[0].shape[3] // HD
    groups = out_ref.shape[1] // (kv_heads * HD)
    tail = last_refs[0].shape[0]
    scale = 1.0 / math.sqrt(HD)
    places = [(p, n) for p in range(parts) for n in range(KNB)]
    swap = lax.broadcasted_iota(jnp.int32, (tail, HD), 0) == tail - 1

    def window(i, lanes):
        values = ahead_refs[i][:, lanes]
        if halo:
            values = jnp.where(at_end, halo_refs[i][:, lanes], values)
        end = jnp.where(swap, last_refs[i][:, lanes], values[SPAN - tail :])
        return [values[: SPAN - tail], end]

    for h in range(kv_heads):
        lanes = slice(h * HD, (h + 1) * HD)
        key = jnp.concatenate([kv_refs[p][n, 0, :, lanes] for p, n in places], 0)
        value = jnp.concatenate([kv_refs[p][n, 1, :, lanes] for p, n in places], 0)
        heads = [slice((h * groups + g) * HD, (h * groups + g + 1) * HD) for g in range(groups)]
        query = jnp.concatenate(sum([window(0, s) for s in heads], []), 0)
        grad = jnp.concatenate(sum([window(1, s) for s in heads], []), 0)
        scores = nt(key, query) * (scale * LOG2E)
        raised = jnp.exp2(scores - jnp.max(scores, axis=0, keepdims=True))
        weights = raised * (1.0 / jnp.sum(raised, axis=0, keepdims=True))
        low = weights.astype(jnp.bfloat16)
        out = nn(value.T, low).T.astype(jnp.bfloat16)
        for g, s in enumerate(heads):
            out_ref[:, s] = out[g * SPAN : (g + 1) * SPAN]
        value_grad = nn(low, grad).astype(jnp.bfloat16)
        slope = nt(value, grad)
        centre = jnp.sum(weights * slope, axis=0, keepdims=True)
        score_grad = (weights * (slope - centre) * scale).astype(jnp.bfloat16)
        key_grad = nn(score_grad, query).astype(jnp.bfloat16)
        for b, (p, n) in enumerate(places):
            grad_refs[p][n, 0, :, lanes] = key_grad[b * rows : (b + 1) * rows]
            grad_refs[p][n, 1, :, lanes] = value_grad[b * rows : (b + 1) * rows]


def shards(cross_query, cross_grad, neighbour_kv, span_neighbours):
    dp_size = lax.axis_size("dp")
    context_size = lax.axis_size("context")
    tensor_size = lax.axis_size("tensor")
    local_rows, _, _, kv_width = neighbour_kv.shape
    width = kv_width // tensor_size
    row_count, query_width = cross_query.shape[1:]
    spans = row_count // SPAN
    count = spans * KNB
    peers = dp_size * tensor_size
    rows = NL // dp_size
    geometry = (local_rows, context_size, tensor_size)
    group = ("dp", "tensor")
    params = pltpu.CompilerParams(vmem_limit_bytes=32 * 1024 * 1024)
    smem = pl.BlockSpec(memory_space=pltpu.SMEM)
    vmem = pl.BlockSpec(memory_space=pltpu.VMEM)

    def ring(array, by):
        return lax.ppermute(array, "dp", [(i, (i + by) % dp_size) for i in range(dp_size)])

    spread = neighbour_kv.transpose(2, 0, 1, 3)
    spread = spread.reshape(SLOTS, local_rows, dp_size, rows, tensor_size, width)
    spread = spread.transpose(2, 4, 0, 1, 3, 5).reshape(peers, SLOTS, local_rows, rows, width)
    ids = lax.dynamic_slice_in_dim(
        span_neighbours, lax.axis_index("context") * spans, spans, 1
    ).reshape(-1)
    ids = jnp.concatenate([ids, lax.axis_index("dp").astype(jnp.int32)[None]])
    query, grad = cross_query[0], cross_grad[0]
    spread, halo_rows = lax.optimization_barrier((spread, (query[:SPAN], grad[:SPAN])))
    held = lax.all_to_all(spread, group, 0, 0, tiled=True)

    back = [(i + 1, i) for i in range(context_size - 1)]
    forth = [(i, i + 1) for i in range(context_size - 1)]
    halo = [lax.ppermute(values, "context", back) for values in halo_rows]

    chunks = CHUNKS
    length = count // chunks
    chunk_rows = row_count // chunks
    part = jax.ShapeDtypeStruct((length, SLOTS, rows, width), jnp.bfloat16)
    delivered = pl.pallas_call(
        functools.partial(deliver_kernel, owners=dp_size, geometry=geometry),
        out_shape=(part,) * (dp_size * chunks),
        in_specs=[smem, vmem],
        out_specs=(vmem,) * (dp_size * chunks),
        compiler_params=params,
        name="deliver",
    )(ids, held)
    order = sorted(range(1, dp_size), key=lambda s: -min(s, dp_size - s))
    tail = 16
    per_chunk = spans // chunks
    block = pl.BlockSpec((SPAN, query_width), lambda w: (w, 0))
    only = pl.BlockSpec((SPAN, query_width), lambda w: (0, 0))
    kv_block = pl.BlockSpec((KNB, SLOTS, rows, width), lambda w: (w, 0, 0, 0))
    kv = []
    for c in range(chunks):
        mine = delivered[c * dp_size : (c + 1) * dp_size]
        arrived = {0: mine[0]}
        for s in order:
            arrived[s] = ring(mine[s], s)
        kv.append([arrived[s] for s in range(dp_size)])
    out_parts = []
    returned = []
    for c in range(chunks):
        ends = c == chunks - 1
        ahead = pl.BlockSpec(
            (SPAN, query_width),
            lambda w, c=c: (jnp.minimum(c * per_chunk + w + 1, spans - 1), 0),
        )
        last = pl.BlockSpec(
            (tail, query_width),
            lambda w, c=c: ((c * per_chunk + w + 1) * (SPAN // tail) - 1, 0),
        )
        out_rows, *kv_grads = pl.pallas_call(
            functools.partial(attention_kernel, parts=dp_size, halo=ends),
            grid=(per_chunk,),
            out_shape=(jax.ShapeDtypeStruct((chunk_rows, query_width), jnp.bfloat16),)
            + (part,) * dp_size,
            in_specs=[ahead, ahead, last, last] + [only] * (2 * ends) + [kv_block] * dp_size,
            out_specs=(block,) + (kv_block,) * dp_size,
            compiler_params=params,
            name="attention",
        )(query, grad, query, grad, *(halo if ends else []), *kv[c])
        out_parts.append(out_rows)
        arrived = {0: kv_grads[0]}
        for s in order:
            arrived[s] = ring(kv_grads[s], -s)
        returned += [arrived[s] for s in range(dp_size)]

    windows = jnp.concatenate(out_parts, 0)
    before = lax.ppermute(windows[row_count - SPAN :], "context", forth)
    position = lax.broadcasted_iota(jnp.int32, windows.shape, 0)
    cross_out = jnp.where(
        position % SPAN == SPAN - 1,
        windows,
        jnp.concatenate([before, windows[: row_count - SPAN]], 0),
    )
    collected = pl.pallas_call(
        functools.partial(collect_kernel, owners=dp_size, geometry=geometry),
        out_shape=jax.ShapeDtypeStruct(held.shape, jnp.bfloat16),
        in_specs=[smem] + [vmem] * (dp_size * chunks),
        out_specs=vmem,
        compiler_params=params,
        name="collect",
    )(ids, *returned)
    final = lax.all_to_all(collected, group, 0, 0, tiled=True)
    final = final.reshape(dp_size, tensor_size, SLOTS, local_rows, rows, width)
    final = final.transpose(3, 0, 4, 2, 1, 5)
    return (cross_out[None], final.reshape(neighbour_kv.shape))


def solution(mesh):
    return jax.shard_map(
        shards,
        mesh=mesh,
        in_specs=(
            P("dp", "context", "tensor"),
            P("dp", "context", "tensor"),
            P(("dp", "context", "tensor"), None, None, None),
            P(),
        ),
        out_specs=(P("dp", "context", "tensor"), P(("dp", "context", "tensor"), None, None, None)),
        check_vma=False,
    )
```

```python
import functools
import math

import jax
import jax.numpy as jnp
from jax import lax
from jax.experimental import pallas as pl
from jax.experimental.pallas import tpu as pltpu
from jax.sharding import PartitionSpec as P

HD = 128
SPAN = 64
NL = 128
KNB = 2
SLOTS = 2
CHUNKS = 2
TAIL = 16
LOG2E = 1.4426950408889634


def nt(a, b):
    return lax.dot_general(a, b, (((1,), (1,)), ((), ())), preferred_element_type=jnp.float32)


def nn(a, b):
    return lax.dot_general(a, b, (((1,), (0,)), ((), ())), preferred_element_type=jnp.float32)


def place_of(row, geometry):
    local_rows, dp_size, context_size, tensor_size = geometry
    device = row // local_rows
    source = device % tensor_size * dp_size + device // (context_size * tensor_size)
    return source, row % local_rows


def deliver_kernel(ids_ref, held_ref, *out_refs, owners, geometry):
    length = out_refs[0].shape[0]
    count = len(out_refs) // owners * length
    me = ids_ref[owners * count]
    for o, out_ref in enumerate(out_refs):
        owner = (me + o % owners) % owners
        for k in range(length):
            row = ids_ref[owner * count + o // owners * length + k]
            source, part = place_of(row, geometry)
            for slot in range(SLOTS):
                out_ref[k, slot] = held_ref[source, slot, part]


def collect_kernel(ids_ref, *refs, owners, geometry):
    held_refs, out_ref = refs[:-1], refs[-1]
    length = held_refs[0].shape[0]
    count = len(held_refs) // owners * length
    me = ids_ref[owners * count]
    for o, held_ref in enumerate(held_refs):
        owner = (me + o % owners) % owners
        for k in range(length):
            row = ids_ref[owner * count + o // owners * length + k]
            source, part = place_of(row, geometry)
            for slot in range(SLOTS):
                out_ref[source, slot, part] = held_ref[k, slot]


def attention_kernel(q_ref, g_ref, *refs, parts, halo, first):
    if halo:
        halo_q_ref, halo_g_ref, *refs = refs
    kv_refs, out_ref, grad_refs = refs[:parts], refs[parts], refs[parts + 1 :]
    rows = kv_refs[0].shape[2]
    kv_heads = kv_refs[0].shape[3] // HD
    groups = out_ref.shape[1] // (kv_heads * HD)
    spans = out_ref.shape[0] // SPAN
    scale = 1.0 / math.sqrt(HD)
    swap = lax.broadcasted_iota(jnp.int32, (TAIL, HD), 0) == TAIL - 1

    def window(ref, halo_ref, span, lanes):
        end = (first + span + 1) * SPAN
        source, start = (halo_ref, 0) if halo and span == spans - 1 else (ref, end)
        stop = start + SPAN - TAIL
        tail = jnp.where(swap, ref[end - TAIL : end, lanes], source[stop : stop + TAIL, lanes])
        return [source[start:stop, lanes], tail]

    def load(span, h):
        places = [(p, span * KNB + n) for p in range(parts) for n in range(KNB)]
        lanes = slice(h * HD, (h + 1) * HD)
        heads = [slice((h * groups + g) * HD, (h * groups + g + 1) * HD) for g in range(groups)]
        key = jnp.concatenate([kv_refs[p][n, 0, :, lanes] for p, n in places], 0)
        value = jnp.concatenate([kv_refs[p][n, 1, :, lanes] for p, n in places], 0)
        halos = (halo_q_ref, halo_g_ref) if halo else (None, None)
        query, grad = (
            jnp.concatenate(sum([window(ref, halo_ref, span, s) for s in heads], []), 0)
            for ref, halo_ref in zip((q_ref, g_ref), halos)
        )
        return places, lanes, heads, key, value, query, grad

    for span in range(spans):
        loaded = [load(span, h) for h in range(kv_heads)]
        all_scores = [nt(key, query) for _, _, _, key, _, query, _ in loaded]
        slopes = [nt(value, grad) for _, _, _, _, value, _, grad in loaded]
        all_weights = []
        for scores in all_scores:
            scores = scores * (scale * LOG2E)
            raised = jnp.exp2(scores - jnp.max(scores, axis=0, keepdims=True))
            all_weights.append(raised * (1.0 / jnp.sum(raised, axis=0, keepdims=True)))
        for (places, lanes, heads, key, value, query, grad), weights, slope in zip(
            loaded, all_weights, slopes
        ):
            low = weights.astype(jnp.bfloat16)
            out = nn(value.T, low).T.astype(jnp.bfloat16)
            for g, s in enumerate(heads):
                out_ref[span * SPAN : (span + 1) * SPAN, s] = out[g * SPAN : (g + 1) * SPAN]
            value_grad = nn(low, grad).astype(jnp.bfloat16)
            centre = jnp.sum(weights * slope, axis=0, keepdims=True)
            score_grad = (weights * (slope - centre) * scale).astype(jnp.bfloat16)
            key_grad = nn(score_grad, query).astype(jnp.bfloat16)
            for b, (p, n) in enumerate(places):
                grad_refs[p][n, 0, :, lanes] = key_grad[b * rows : (b + 1) * rows]
                grad_refs[p][n, 1, :, lanes] = value_grad[b * rows : (b + 1) * rows]


def shards(cross_query, cross_grad, neighbour_kv, span_neighbours):
    dp_size = lax.axis_size("dp")
    context_size = lax.axis_size("context")
    tensor_size = lax.axis_size("tensor")
    local_rows, _, _, kv_width = neighbour_kv.shape
    width = kv_width // tensor_size
    row_count, query_width = cross_query.shape[1:]
    spans = row_count // SPAN
    count = spans * KNB
    peers = dp_size * tensor_size
    rows = NL // dp_size
    geometry = (local_rows, dp_size, context_size, tensor_size)
    group = ("tensor", "dp")
    params = pltpu.CompilerParams(vmem_limit_bytes=8 * 1024 * 1024)
    smem = pl.BlockSpec(memory_space=pltpu.SMEM)
    vmem = pl.BlockSpec(memory_space=pltpu.VMEM)

    def ring(array, by):
        return lax.ppermute(array, "dp", [(i, (i + by) % dp_size) for i in range(dp_size)])

    spread = neighbour_kv.transpose(2, 0, 1, 3)
    spread = spread.reshape(SLOTS, local_rows, dp_size, rows, tensor_size, width)
    spread = spread.transpose(4, 2, 0, 1, 3, 5).reshape(peers, SLOTS, local_rows, rows, width)
    ids = lax.dynamic_slice_in_dim(
        span_neighbours, lax.axis_index("context") * spans, spans, 1
    ).reshape(-1)
    ids = jnp.concatenate([ids, lax.axis_index("dp").astype(jnp.int32)[None]])
    query, grad = cross_query[0], cross_grad[0]
    spread, query, grad = lax.optimization_barrier((spread, query, grad))
    held = lax.all_to_all(spread, group, 0, 0, tiled=True)

    back = [(i + 1, i) for i in range(context_size - 1)]
    forth = [(i, i + 1) for i in range(context_size - 1)]
    halo = [lax.ppermute(values[:SPAN], "context", back) for values in (query, grad)]

    chunks = CHUNKS
    length = count // chunks
    chunk_rows = row_count // chunks
    part = jax.ShapeDtypeStruct((length, SLOTS, rows, width), jnp.bfloat16)
    delivered = pl.pallas_call(
        functools.partial(deliver_kernel, owners=dp_size, geometry=geometry),
        out_shape=(part,) * (dp_size * chunks),
        in_specs=[smem, vmem],
        out_specs=(vmem,) * (dp_size * chunks),
        compiler_params=params,
        name="deliver",
    )(ids, held)
    order = sorted(range(1, dp_size), key=lambda s: -min(s, dp_size - s))
    kv = []
    for c in range(chunks):
        mine = delivered[c * dp_size : (c + 1) * dp_size]
        arrived = {0: mine[0]}
        for s in order:
            arrived[s] = ring(mine[s], s)
        kv.append([arrived[s] for s in range(dp_size)])
    out_parts = []
    returned = []
    for c in range(chunks):
        ends = c == chunks - 1
        operands = [query, grad] + (halo if ends else []) + kv[c]
        out_rows, *kv_grads = pl.pallas_call(
            functools.partial(
                attention_kernel, parts=dp_size, halo=ends, first=c * spans // chunks
            ),
            out_shape=(jax.ShapeDtypeStruct((chunk_rows, query_width), jnp.bfloat16),)
            + (part,) * dp_size,
            in_specs=[vmem] * len(operands),
            out_specs=(vmem,) * (1 + dp_size),
            compiler_params=pltpu.CompilerParams(vmem_limit_bytes=16 * 1024 * 1024),
            name="attention",
        )(*operands)
        out_parts.append(out_rows)
        arrived = {0: kv_grads[0]}
        for s in order:
            arrived[s] = ring(kv_grads[s], -s)
        returned += [arrived[s] for s in range(dp_size)]

    windows = jnp.concatenate(out_parts, 0)
    before = lax.ppermute(windows[row_count - SPAN :], "context", forth)
    position = lax.broadcasted_iota(jnp.int32, windows.shape, 0)
    cross_out = jnp.where(
        position % SPAN == SPAN - 1,
        windows,
        jnp.concatenate([before, windows[: row_count - SPAN]], 0),
    )
    collected = pl.pallas_call(
        functools.partial(collect_kernel, owners=dp_size, geometry=geometry),
        out_shape=jax.ShapeDtypeStruct(held.shape, jnp.bfloat16),
        in_specs=[smem] + [vmem] * (dp_size * chunks),
        out_specs=vmem,
        compiler_params=params,
        name="collect",
    )(ids, *returned)
    final = lax.all_to_all(collected, group, 0, 0, tiled=True)
    final = final.reshape(tensor_size, dp_size, SLOTS, local_rows, rows, width)
    final = final.transpose(3, 1, 4, 2, 0, 5)
    return (cross_out[None], final.reshape(neighbour_kv.shape))


def solution(mesh):
    return jax.shard_map(
        shards,
        mesh=mesh,
        in_specs=(
            P("dp", "context", "tensor"),
            P("dp", "context", "tensor"),
            P(("dp", "context", "tensor"), None, None, None),
            P(),
        ),
        out_specs=(P("dp", "context", "tensor"), P(("dp", "context", "tensor"), None, None, None)),
        check_vma=False,
    )
```

```python
import functools
import math

import jax
import jax.numpy as jnp
from jax import lax
from jax.experimental import pallas as pl
from jax.experimental.pallas import tpu as pltpu
from jax.sharding import PartitionSpec as P

HD = 128
SPAN = 64
NL = 128
KNB = 2
SLOTS = 2
CHUNKS = (2, 2)
TAIL = 16
LOG2E = 1.4426950408889634


def nt(a, b):
    return lax.dot_general(a, b, (((1,), (1,)), ((), ())), preferred_element_type=jnp.float32)


def nn(a, b):
    return lax.dot_general(a, b, (((1,), (0,)), ((), ())), preferred_element_type=jnp.float32)


def place_of(row, geometry):
    local_rows, dp_size, context_size, tensor_size = geometry
    device = row // local_rows
    source = device % tensor_size * dp_size + device // (context_size * tensor_size)
    return source, row % local_rows


def listed_places(ids_ref, blocks, owners, geometry):
    lengths = [block.shape[0] for block in blocks[::owners]]
    me = ids_ref[owners * sum(lengths)]
    for o, block in enumerate(blocks):
        start = (me + o % owners) % owners * sum(lengths) + sum(lengths[: o // owners])
        for k in range(block.shape[0]):
            yield block, k, place_of(ids_ref[start + k], geometry)


def deliver_kernel(ids_ref, held_ref, *out_refs, owners, geometry):
    for block, k, (source, part) in listed_places(ids_ref, out_refs, owners, geometry):
        for slot in range(SLOTS):
            block[k, slot] = held_ref[source, slot, part]


def collect_kernel(ids_ref, *refs, owners, geometry):
    *held_refs, out_ref, sem = refs
    copies = [
        pltpu.make_async_copy(block.at[k], out_ref.at[source, :, part], sem.at[i])
        for i, (block, k, (source, part)) in enumerate(
            listed_places(ids_ref, held_refs, owners, geometry)
        )
    ]
    for copy in copies:
        copy.start()
    for copy in copies:
        copy.wait()


def attention_kernel(q_ref, g_ref, *refs, parts, halo, first):
    if halo:
        *sources, refs = refs[0], refs[1], refs[2:]
        *refs, halo_q_ref, halo_g_ref, sem = refs
        copies = [
            pltpu.make_async_copy(source, target, sem.at[i])
            for i, (source, target) in enumerate(zip(sources, (halo_q_ref, halo_g_ref)))
        ]
        for copy in copies:
            copy.start()
    kv_refs, out_ref, grad_refs = refs[:parts], refs[parts], refs[parts + 1 :]
    rows = kv_refs[0].shape[2]
    kv_heads = kv_refs[0].shape[3] // HD
    groups = out_ref.shape[1] // (kv_heads * HD)
    spans = out_ref.shape[0] // SPAN
    scale = 1.0 / math.sqrt(HD)
    swap = lax.broadcasted_iota(jnp.int32, (TAIL, HD), 0) == TAIL - 1

    def window(ref, halo_ref, span, lanes):
        end = (first + span + 1) * SPAN
        source, start = (halo_ref, 0) if halo and span == spans - 1 else (ref, end)
        stop = start + SPAN - TAIL
        tail = jnp.where(swap, ref[end - TAIL : end, lanes], source[stop : stop + TAIL, lanes])
        return [source[start:stop, lanes], tail]

    def load(span, h):
        places = [(p, span * KNB + n) for p in range(parts) for n in range(KNB)]
        lanes = slice(h * HD, (h + 1) * HD)
        heads = [slice((h * groups + g) * HD, (h * groups + g + 1) * HD) for g in range(groups)]
        key = jnp.concatenate([kv_refs[p][n, 0, :, lanes] for p, n in places], 0)
        value = jnp.concatenate([kv_refs[p][n, 1, :, lanes] for p, n in places], 0)
        halos = (halo_q_ref, halo_g_ref) if halo else (None, None)
        query, grad = (
            jnp.concatenate(sum([window(ref, halo_ref, span, s) for s in heads], []), 0)
            for ref, halo_ref in zip((q_ref, g_ref), halos)
        )
        return places, lanes, heads, key, value, query, grad

    for span in range(spans):
        if halo and span == spans - 1:
            for copy in copies:
                copy.wait()
        loaded = [load(span, h) for h in range(kv_heads)]
        all_scores = [nt(key, query) for _, _, _, key, _, query, _ in loaded]
        slopes = [nt(value, grad) for _, _, _, _, value, _, grad in loaded]
        all_weights = []
        for scores in all_scores:
            scores = scores * (scale * LOG2E)
            raised = jnp.exp2(scores - jnp.max(scores, axis=0, keepdims=True))
            all_weights.append(raised * (1.0 / jnp.sum(raised, axis=0, keepdims=True)))
        for (places, lanes, heads, key, value, query, grad), weights, slope in zip(
            loaded, all_weights, slopes
        ):
            low = weights.astype(jnp.bfloat16)
            out = nn(value.T, low).T.astype(jnp.bfloat16)
            for g, s in enumerate(heads):
                out_ref[span * SPAN : (span + 1) * SPAN, s] = out[g * SPAN : (g + 1) * SPAN]
            value_grad = nn(low, grad).astype(jnp.bfloat16)
            centre = jnp.sum(weights * slope, axis=0, keepdims=True)
            score_grad = (weights * (slope - centre) * scale).astype(jnp.bfloat16)
            key_grad = nn(score_grad, query).astype(jnp.bfloat16)
            for b, (p, n) in enumerate(places):
                grad_refs[p][n, 0, :, lanes] = key_grad[b * rows : (b + 1) * rows]
                grad_refs[p][n, 1, :, lanes] = value_grad[b * rows : (b + 1) * rows]


def shards(cross_query, cross_grad, neighbour_kv, span_neighbours):
    dp_size = lax.axis_size("dp")
    context_size = lax.axis_size("context")
    tensor_size = lax.axis_size("tensor")
    local_rows, _, _, kv_width = neighbour_kv.shape
    width = kv_width // tensor_size
    row_count, query_width = cross_query.shape[1:]
    spans = row_count // SPAN
    count = spans * KNB
    peers = dp_size * tensor_size
    rows = NL // dp_size
    geometry = (local_rows, dp_size, context_size, tensor_size)
    group = ("tensor", "dp")
    params = pltpu.CompilerParams(vmem_limit_bytes=8 * 1024 * 1024)
    smem = pl.BlockSpec(memory_space=pltpu.SMEM)
    vmem = pl.BlockSpec(memory_space=pltpu.VMEM)

    def ring(array, by):
        return lax.ppermute(array, "dp", [(i, (i + by) % dp_size) for i in range(dp_size)])

    spread = neighbour_kv.transpose(2, 0, 1, 3)
    spread = spread.reshape(SLOTS, local_rows, dp_size, rows, tensor_size, width)
    spread = spread.transpose(4, 2, 0, 1, 3, 5).reshape(peers, SLOTS, local_rows, rows, width)
    ids = lax.dynamic_slice_in_dim(
        span_neighbours, lax.axis_index("context") * spans, spans, 1
    ).reshape(-1)
    ids = jnp.concatenate([ids, lax.axis_index("dp").astype(jnp.int32)[None]])
    query, grad = cross_query[0], cross_grad[0]
    spread, query, grad = lax.optimization_barrier((spread, query, grad))
    held = lax.all_to_all(spread, group, 0, 0, tiled=True)

    back = [(i + 1, i) for i in range(context_size - 1)]
    forth = [(i, i + 1) for i in range(context_size - 1)]
    halo = [lax.ppermute(values[:SPAN], "context", back) for values in (query, grad)]

    chunks = CHUNKS if sum(CHUNKS) == spans else (spans,)
    parts = [
        jax.ShapeDtypeStruct((n * KNB, SLOTS, rows, width), jnp.bfloat16)
        for n in chunks
        for _ in range(dp_size)
    ]
    delivered = pl.pallas_call(
        functools.partial(deliver_kernel, owners=dp_size, geometry=geometry),
        out_shape=parts,
        in_specs=[smem, vmem],
        out_specs=[vmem] * len(parts),
        compiler_params=params,
        name="deliver",
    )(ids, held)
    order = sorted(range(1, dp_size), key=lambda s: -min(s, dp_size - s))
    kv = []
    for c in range(len(chunks)):
        mine = delivered[c * dp_size : (c + 1) * dp_size]
        arrived = {0: mine[0]}
        for s in order:
            arrived[s] = ring(mine[s], s)
        kv.append([arrived[s] for s in range(dp_size)])
    out_parts = []
    returned = []
    for c, n in enumerate(chunks):
        ends = c == len(chunks) - 1
        halo_rows = halo if ends else []
        anywhere = pl.BlockSpec(memory_space=pl.ANY)
        scratch = [pltpu.VMEM((SPAN, query_width), jnp.bfloat16)] * 2
        scratch.append(pltpu.SemaphoreType.DMA((2,)))
        out_rows, *kv_grads = pl.pallas_call(
            functools.partial(
                attention_kernel, parts=dp_size, halo=ends, first=sum(chunks[:c])
            ),
            out_shape=[jax.ShapeDtypeStruct((n * SPAN, query_width), jnp.bfloat16)]
            + parts[c * dp_size : (c + 1) * dp_size],
            in_specs=[vmem] * 2 + [anywhere] * len(halo_rows) + [vmem] * dp_size,
            out_specs=[vmem] * (1 + dp_size),
            scratch_shapes=scratch if ends else [],
            compiler_params=pltpu.CompilerParams(vmem_limit_bytes=16 * 1024 * 1024),
            name="attention",
        )(query, grad, *halo_rows, *kv[c])
        out_parts.append(out_rows)
        arrived = {0: kv_grads[0]}
        for s in order:
            arrived[s] = ring(kv_grads[s], -s)
        returned += [arrived[s] for s in range(dp_size)]

    windows = jnp.concatenate(out_parts, 0)
    before = lax.ppermute(windows[row_count - SPAN :], "context", forth)
    position = lax.broadcasted_iota(jnp.int32, windows.shape, 0)
    cross_out = jnp.where(
        position % SPAN == SPAN - 1,
        windows,
        jnp.concatenate([before, windows[: row_count - SPAN]], 0),
    )
    collected = pl.pallas_call(
        functools.partial(collect_kernel, owners=dp_size, geometry=geometry),
        out_shape=jax.ShapeDtypeStruct(held.shape, jnp.bfloat16),
        in_specs=[smem] + [vmem] * len(returned),
        out_specs=pl.BlockSpec(memory_space=pl.ANY),
        scratch_shapes=[pltpu.SemaphoreType.DMA((dp_size * count,))],
        compiler_params=params,
        name="collect",
    )(ids, *returned)
    final = lax.all_to_all(collected, group, 0, 0, tiled=True)
    final = final.reshape(tensor_size, dp_size, SLOTS, local_rows, rows, width)
    final = final.transpose(3, 1, 4, 2, 0, 5)
    return (cross_out[None], final.reshape(neighbour_kv.shape))


def solution(mesh):
    return jax.shard_map(
        shards,
        mesh=mesh,
        in_specs=(
            P("dp", "context", "tensor"),
            P("dp", "context", "tensor"),
            P(("dp", "context", "tensor"), None, None, None),
            P(),
        ),
        out_specs=(P("dp", "context", "tensor"), P(("dp", "context", "tensor"), None, None, None)),
        check_vma=False,
    )
```

```python
import functools
import math

import jax
import jax.numpy as jnp
from jax import lax
from jax.experimental import pallas as pl
from jax.experimental.pallas import tpu as pltpu
from jax.sharding import PartitionSpec as P

HD = 128
SPAN = 64
NL = 128
KNB = 2
SLOTS = 2
CHUNKS = (2, 2)
TAIL = 16
LOG2E = 1.4426950408889634


def nt(a, b):
    return lax.dot_general(a, b, (((1,), (1,)), ((), ())), preferred_element_type=jnp.float32)


def nn(a, b):
    return lax.dot_general(a, b, (((1,), (0,)), ((), ())), preferred_element_type=jnp.float32)


def place_of(row, geometry):
    local_rows, dp_size, context_size, tensor_size = geometry
    device = row // local_rows
    source = device % tensor_size * dp_size + device // (context_size * tensor_size)
    return source, row % local_rows


def listed_places(ids_ref, blocks, owners, geometry, first, count):
    lengths = [block.shape[0] for block in blocks[::owners]]
    me = ids_ref[owners * count]
    for o, block in enumerate(blocks):
        start = (me + o % owners) % owners * count + first + sum(lengths[: o // owners])
        for k in range(block.shape[0]):
            yield block, k, place_of(ids_ref[start + k], geometry)


def deliver_kernel(ids_ref, held_ref, *out_refs, owners, geometry, count):
    for block, k, (source, part) in listed_places(
        ids_ref, out_refs, owners, geometry, 0, count
    ):
        for slot in range(SLOTS):
            block[k, slot] = held_ref[source, slot, part]


def collect_kernel(ids_ref, *refs, owners, geometry, first, count):
    held_refs, (out_ref, sem) = refs[:owners], refs[-2:]
    copies = [
        pltpu.make_async_copy(block.at[k], out_ref.at[source, :, part], sem.at[i])
        for i, (block, k, (source, part)) in enumerate(
            listed_places(ids_ref, held_refs, owners, geometry, first, count)
        )
    ]
    for copy in copies:
        copy.start()
    for copy in copies:
        copy.wait()


def attention_kernel(q_ref, g_ref, *refs, parts, halo, first):
    if halo:
        *sources, refs = refs[0], refs[1], refs[2:]
        *refs, halo_q_ref, halo_g_ref, sem = refs
        copies = [
            pltpu.make_async_copy(source, target, sem.at[i])
            for i, (source, target) in enumerate(zip(sources, (halo_q_ref, halo_g_ref)))
        ]
        for copy in copies:
            copy.start()
    kv_refs, out_ref, grad_refs = refs[:parts], refs[parts], refs[parts + 1 :]
    rows = kv_refs[0].shape[2]
    kv_heads = kv_refs[0].shape[3] // HD
    groups = out_ref.shape[1] // (kv_heads * HD)
    spans = out_ref.shape[0] // SPAN
    scale = 1.0 / math.sqrt(HD)
    swap = lax.broadcasted_iota(jnp.int32, (TAIL, HD), 0) == TAIL - 1

    def window(ref, halo_ref, span, lanes):
        end = (first + span + 1) * SPAN
        source, start = (halo_ref, 0) if halo and span == spans - 1 else (ref, end)
        stop = start + SPAN - TAIL
        tail = jnp.where(swap, ref[end - TAIL : end, lanes], source[stop : stop + TAIL, lanes])
        return [source[start:stop, lanes], tail]

    def load(span, h):
        places = [(p, span * KNB + n) for p in range(parts) for n in range(KNB)]
        lanes = slice(h * HD, (h + 1) * HD)
        heads = [slice((h * groups + g) * HD, (h * groups + g + 1) * HD) for g in range(groups)]
        key = jnp.concatenate([kv_refs[p][n, 0, :, lanes] for p, n in places], 0)
        value = jnp.concatenate([kv_refs[p][n, 1, :, lanes] for p, n in places], 0)
        halos = (halo_q_ref, halo_g_ref) if halo else (None, None)
        query, grad = (
            jnp.concatenate(sum([window(ref, halo_ref, span, s) for s in heads], []), 0)
            for ref, halo_ref in zip((q_ref, g_ref), halos)
        )
        return places, lanes, heads, key, value, query, grad

    stages = [range(spans - 1), range(spans - 1, spans)] if halo else [range(spans)]
    for stage in stages:
        if halo and spans - 1 in stage:
            for copy in copies:
                copy.wait()
        loaded = [(span,) + load(span, h) for span in stage for h in range(kv_heads)]
        all_scores = [nt(key, query) for *_, key, _, query, _ in loaded]
        slopes = [nt(value, grad) for *_, value, _, grad in loaded]
        all_raised = [
            jnp.exp2((scores - jnp.max(scores, axis=0, keepdims=True)) * (scale * LOG2E))
            for scores in all_scores
        ]
        shares = [1.0 / jnp.sum(raised, axis=0, keepdims=True) for raised in all_raised]
        for (span, places, lanes, heads, _, value, query, grad), raised, share, slope in zip(
            loaded, all_raised, shares, slopes
        ):
            low = (raised * share).astype(jnp.bfloat16)
            out = nn(value.T, low).T.astype(jnp.bfloat16)
            for g, s in enumerate(heads):
                out_ref[span * SPAN : (span + 1) * SPAN, s] = out[g * SPAN : (g + 1) * SPAN]
            value_grad = nn(low, grad).astype(jnp.bfloat16)
            centre = jnp.sum(raised * slope, axis=0, keepdims=True) * share
            score_grad = (raised * (share * scale) * (slope - centre)).astype(jnp.bfloat16)
            key_grad = nn(score_grad, query).astype(jnp.bfloat16)
            for b, (p, n) in enumerate(places):
                grad_refs[p][n, 0, :, lanes] = key_grad[b * rows : (b + 1) * rows]
                grad_refs[p][n, 1, :, lanes] = value_grad[b * rows : (b + 1) * rows]


def shards(cross_query, cross_grad, neighbour_kv, span_neighbours):
    dp_size = lax.axis_size("dp")
    context_size = lax.axis_size("context")
    tensor_size = lax.axis_size("tensor")
    local_rows, _, _, kv_width = neighbour_kv.shape
    width = kv_width // tensor_size
    row_count, query_width = cross_query.shape[1:]
    spans = row_count // SPAN
    count = spans * KNB
    peers = dp_size * tensor_size
    rows = NL // dp_size
    geometry = (local_rows, dp_size, context_size, tensor_size)
    group = ("tensor", "dp")
    params = pltpu.CompilerParams(vmem_limit_bytes=8 * 1024 * 1024)
    smem = pl.BlockSpec(memory_space=pltpu.SMEM)
    vmem = pl.BlockSpec(memory_space=pltpu.VMEM)

    def ring(array, by):
        return lax.ppermute(array, "dp", [(i, (i + by) % dp_size) for i in range(dp_size)])

    spread = neighbour_kv.transpose(2, 0, 1, 3)
    spread = spread.reshape(SLOTS, local_rows, dp_size, rows, tensor_size, width)
    spread = spread.transpose(4, 2, 0, 1, 3, 5).reshape(peers, SLOTS, local_rows, rows, width)
    ids = lax.dynamic_slice_in_dim(
        span_neighbours, lax.axis_index("context") * spans, spans, 1
    ).reshape(-1)
    ids = jnp.concatenate([ids, lax.axis_index("dp").astype(jnp.int32)[None]])
    query, grad = cross_query[0], cross_grad[0]
    spread, query, grad = lax.optimization_barrier((spread, query, grad))
    held = lax.all_to_all(spread, group, 0, 0, tiled=True)

    back = [(i + 1, i) for i in range(context_size - 1)]
    forth = [(i, i + 1) for i in range(context_size - 1)]
    halo = [lax.ppermute(values[:SPAN], "context", back) for values in (query, grad)]

    chunks = CHUNKS if sum(CHUNKS) == spans else (spans,)
    parts = [
        jax.ShapeDtypeStruct((n * KNB, SLOTS, rows, width), jnp.bfloat16)
        for n in chunks
        for _ in range(dp_size)
    ]
    delivered = pl.pallas_call(
        functools.partial(deliver_kernel, owners=dp_size, geometry=geometry, count=count),
        out_shape=parts,
        in_specs=[smem, vmem],
        out_specs=[vmem] * len(parts),
        compiler_params=params,
        name="deliver",
    )(ids, held)
    order = sorted(range(1, dp_size), key=lambda s: -min(s, dp_size - s))
    kv = []
    for c in range(len(chunks)):
        mine = delivered[c * dp_size : (c + 1) * dp_size]
        arrived = {0: mine[0]}
        for s in order:
            arrived[s] = ring(mine[s], s)
        kv.append([arrived[s] for s in range(dp_size)])
    out_parts = []
    returned = []
    for c, n in enumerate(chunks):
        ends = c == len(chunks) - 1
        halo_rows = halo if ends else []
        anywhere = pl.BlockSpec(memory_space=pl.ANY)
        scratch = [pltpu.VMEM((SPAN, query_width), jnp.bfloat16)] * 2
        scratch.append(pltpu.SemaphoreType.DMA((2,)))
        out_rows, *kv_grads = pl.pallas_call(
            functools.partial(
                attention_kernel, parts=dp_size, halo=ends, first=sum(chunks[:c])
            ),
            out_shape=[jax.ShapeDtypeStruct((n * SPAN, query_width), jnp.bfloat16)]
            + parts[c * dp_size : (c + 1) * dp_size],
            in_specs=[vmem] * 2 + [anywhere] * len(halo_rows) + [vmem] * dp_size,
            out_specs=[vmem] * (1 + dp_size),
            scratch_shapes=scratch if ends else [],
            compiler_params=pltpu.CompilerParams(vmem_limit_bytes=16 * 1024 * 1024),
            name="attention",
        )(query, grad, *halo_rows, *kv[c])
        out_parts.append(out_rows)
        arrived = {0: kv_grads[0]}
        for s in order:
            arrived[s] = ring(kv_grads[s], -s)
        returned.append([arrived[s] for s in range(dp_size)])

    windows = jnp.concatenate(out_parts, 0)
    before = lax.ppermute(windows[row_count - SPAN :], "context", forth)
    position = lax.broadcasted_iota(jnp.int32, windows.shape, 0)
    cross_out = jnp.where(
        position % SPAN == SPAN - 1,
        windows,
        jnp.concatenate([before, windows[: row_count - SPAN]], 0),
    )
    collected = []
    for c in reversed(range(len(chunks))):
        collected = [
            pl.pallas_call(
                functools.partial(
                    collect_kernel,
                    owners=dp_size,
                    geometry=geometry,
                    first=sum(chunks[:c]) * KNB,
                    count=count,
                ),
                out_shape=jax.ShapeDtypeStruct(held.shape, jnp.bfloat16),
                in_specs=[smem] + [vmem] * dp_size + [anywhere] * len(collected),
                out_specs=anywhere,
                scratch_shapes=[pltpu.SemaphoreType.DMA((dp_size * chunks[c] * KNB,))],
                input_output_aliases={1 + dp_size: 0} if collected else {},
                compiler_params=params,
                name="collect",
            )(ids, *returned[c], *collected)
        ]
    final = lax.all_to_all(collected[0], group, 0, 0, tiled=True)
    final = final.reshape(tensor_size, dp_size, SLOTS, local_rows, rows, width)
    final = final.transpose(3, 1, 4, 2, 0, 5)
    return (cross_out[None], final.reshape(neighbour_kv.shape))


def solution(mesh):
    return jax.shard_map(
        shards,
        mesh=mesh,
        in_specs=(
            P("dp", "context", "tensor"),
            P("dp", "context", "tensor"),
            P(("dp", "context", "tensor"), None, None, None),
            P(),
        ),
        out_specs=(P("dp", "context", "tensor"), P(("dp", "context", "tensor"), None, None, None)),
        check_vma=False,
    )
```

```python
import functools
import math

import jax
import jax.numpy as jnp
from jax import lax
from jax.experimental import pallas as pl
from jax.experimental.pallas import tpu as pltpu
from jax.sharding import PartitionSpec as P

HD = 128
SPAN = 64
NL = 128
KNB = 2
SLOTS = 2
CHUNKS = (2, 2)
TAIL = 16
LOG2E = 1.4426950408889634


def nt(a, b):
    return lax.dot_general(a, b, (((1,), (1,)), ((), ())), preferred_element_type=jnp.float32)


def nn(a, b):
    return lax.dot_general(a, b, (((1,), (0,)), ((), ())), preferred_element_type=jnp.float32)


def split(value, size):
    if size & (size - 1) == 0:
        return lax.shift_right_logical(value, size.bit_length() - 1), value & (size - 1)
    return lax.div(value, size), lax.rem(value, size)


def place_of(row, geometry):
    local_rows, dp_size, context_size, tensor_size = geometry
    device, part = split(row, local_rows)
    tensor = split(device, tensor_size)[1]
    dp = split(device, context_size * tensor_size)[0]
    return tensor * dp_size + dp, part


def listed_places(ids_ref, blocks, owners, geometry, first, count):
    lengths = [block.shape[0] for block in blocks[::owners]]
    me = ids_ref[owners * count]
    for o, block in enumerate(blocks):
        start = split(me + o % owners, owners)[1] * count + first + sum(lengths[: o // owners])
        for k in range(block.shape[0]):
            yield block, k, place_of(ids_ref[start + k], geometry)


def deliver_kernel(ids_ref, held_ref, *out_refs, owners, geometry, count):
    for block, k, (source, part) in listed_places(
        ids_ref, out_refs, owners, geometry, 0, count
    ):
        for slot in range(SLOTS):
            block[k, slot] = held_ref[source, slot, part]


def collect_kernel(ids_ref, *refs, owners, geometry, first, count):
    held_refs, (out_ref, sem) = refs[:owners], refs[-2:]
    copies = [
        pltpu.make_async_copy(block.at[k], out_ref.at[source, :, part], sem.at[i])
        for i, (block, k, (source, part)) in enumerate(
            listed_places(ids_ref, held_refs, owners, geometry, first, count)
        )
    ]
    for copy in copies:
        copy.start()
    for copy in copies:
        copy.wait()


def attention_kernel(q_ref, g_ref, *refs, parts, halo, first):
    if halo:
        *sources, refs = refs[0], refs[1], refs[2:]
        *refs, halo_q_ref, halo_g_ref, sem = refs
        copies = [
            pltpu.make_async_copy(source, target, sem.at[i])
            for i, (source, target) in enumerate(zip(sources, (halo_q_ref, halo_g_ref)))
        ]
        for copy in copies:
            copy.start()
    kv_refs, out_ref, grad_refs = refs[:parts], refs[parts], refs[parts + 1 :]
    rows = kv_refs[0].shape[2]
    kv_heads = kv_refs[0].shape[3] // HD
    groups = out_ref.shape[1] // (kv_heads * HD)
    spans = out_ref.shape[0] // SPAN
    scale = 1.0 / math.sqrt(HD)
    swap = lax.broadcasted_iota(jnp.int32, (TAIL, HD), 0) == TAIL - 1

    def window(ref, halo_ref, span, lanes):
        end = (first + span + 1) * SPAN
        source, start = (halo_ref, 0) if halo and span == spans - 1 else (ref, end)
        stop = start + SPAN - TAIL
        tail = jnp.where(swap, ref[end - TAIL : end, lanes], source[stop : stop + TAIL, lanes])
        return [source[start:stop, lanes], tail]

    def load(span, h):
        places = [(p, span * KNB + n) for p in range(parts) for n in range(KNB)]
        lanes = slice(h * HD, (h + 1) * HD)
        heads = [slice((h * groups + g) * HD, (h * groups + g + 1) * HD) for g in range(groups)]
        key = jnp.concatenate([kv_refs[p][n, 0, :, lanes] for p, n in places], 0)
        value = jnp.concatenate([kv_refs[p][n, 1, :, lanes] for p, n in places], 0)
        halos = (halo_q_ref, halo_g_ref) if halo else (None, None)
        query, grad = (
            jnp.concatenate(sum([window(ref, halo_ref, span, s) for s in heads], []), 0)
            for ref, halo_ref in zip((q_ref, g_ref), halos)
        )
        return places, lanes, heads, key, value, query, grad

    stages = [range(spans - 1), range(spans - 1, spans)] if halo else [range(spans)]
    for stage in stages:
        if halo and spans - 1 in stage:
            for copy in copies:
                copy.wait()
        loaded = [(span,) + load(span, h) for span in stage for h in range(kv_heads)]
        all_scores = [nt(key, query) for *_, key, _, query, _ in loaded]
        slopes = [nt(value, grad) for *_, value, _, grad in loaded]
        all_raised = [
            jnp.exp2((scores - jnp.max(scores, axis=0, keepdims=True)) * (scale * LOG2E))
            for scores in all_scores
        ]
        shares = [1.0 / jnp.sum(raised, axis=0, keepdims=True) for raised in all_raised]
        for (span, places, lanes, heads, _, value, query, grad), raised, share, slope in zip(
            loaded, all_raised, shares, slopes
        ):
            low = (raised * share).astype(jnp.bfloat16)
            out = nn(value.T, low).T.astype(jnp.bfloat16)
            for g, s in enumerate(heads):
                out_ref[span * SPAN : (span + 1) * SPAN, s] = out[g * SPAN : (g + 1) * SPAN]
            value_grad = nn(low, grad).astype(jnp.bfloat16)
            centre = jnp.sum(raised * slope, axis=0, keepdims=True) * share
            score_grad = (raised * (share * scale) * (slope - centre)).astype(jnp.bfloat16)
            key_grad = nn(score_grad, query).astype(jnp.bfloat16)
            for b, (p, n) in enumerate(places):
                grad_refs[p][n, 0, :, lanes] = key_grad[b * rows : (b + 1) * rows]
                grad_refs[p][n, 1, :, lanes] = value_grad[b * rows : (b + 1) * rows]


def shards(cross_query, cross_grad, neighbour_kv, span_neighbours):
    dp_size = lax.axis_size("dp")
    context_size = lax.axis_size("context")
    tensor_size = lax.axis_size("tensor")
    local_rows, _, _, kv_width = neighbour_kv.shape
    width = kv_width // tensor_size
    row_count, query_width = cross_query.shape[1:]
    spans = row_count // SPAN
    count = spans * KNB
    peers = dp_size * tensor_size
    rows = NL // dp_size
    geometry = (local_rows, dp_size, context_size, tensor_size)
    group = ("tensor", "dp")
    params = pltpu.CompilerParams(vmem_limit_bytes=8 * 1024 * 1024)
    smem = pl.BlockSpec(memory_space=pltpu.SMEM)
    vmem = pl.BlockSpec(memory_space=pltpu.VMEM)

    def ring(array, by):
        return lax.ppermute(array, "dp", [(i, (i + by) % dp_size) for i in range(dp_size)])

    spread = neighbour_kv.transpose(2, 0, 1, 3)
    spread = spread.reshape(SLOTS, local_rows, dp_size, rows, tensor_size, width)
    spread = spread.transpose(4, 2, 0, 1, 3, 5).reshape(peers, SLOTS, local_rows, rows, width)
    ids = lax.dynamic_slice_in_dim(
        span_neighbours, lax.axis_index("context") * spans, spans, 1
    ).reshape(-1)
    ids = jnp.concatenate([ids, lax.axis_index("dp").astype(jnp.int32)[None]])
    query, grad = cross_query[0], cross_grad[0]
    spread, query, grad = lax.optimization_barrier((spread, query, grad))
    held = lax.all_to_all(spread, group, 0, 0, tiled=True)

    back = [(i + 1, i) for i in range(context_size - 1)]
    forth = [(i, i + 1) for i in range(context_size - 1)]
    halo = [lax.ppermute(values[:SPAN], "context", back) for values in (query, grad)]

    chunks = CHUNKS if sum(CHUNKS) == spans else (spans,)
    parts = [
        jax.ShapeDtypeStruct((n * KNB, SLOTS, rows, width), jnp.bfloat16)
        for n in chunks
        for _ in range(dp_size)
    ]
    delivered = pl.pallas_call(
        functools.partial(deliver_kernel, owners=dp_size, geometry=geometry, count=count),
        out_shape=parts,
        in_specs=[smem, vmem],
        out_specs=[vmem] * len(parts),
        compiler_params=params,
        name="deliver",
    )(ids, held)
    order = sorted(range(1, dp_size), key=lambda s: -min(s, dp_size - s))
    kv = []
    for c in range(len(chunks)):
        mine = delivered[c * dp_size : (c + 1) * dp_size]
        arrived = {0: mine[0]}
        for s in order:
            arrived[s] = ring(mine[s], s)
        kv.append([arrived[s] for s in range(dp_size)])
    out_parts = []
    returned = []
    for c, n in enumerate(chunks):
        ends = c == len(chunks) - 1
        halo_rows = halo if ends else []
        anywhere = pl.BlockSpec(memory_space=pl.ANY)
        scratch = [pltpu.VMEM((SPAN, query_width), jnp.bfloat16)] * 2
        scratch.append(pltpu.SemaphoreType.DMA((2,)))
        out_rows, *kv_grads = pl.pallas_call(
            functools.partial(
                attention_kernel, parts=dp_size, halo=ends, first=sum(chunks[:c])
            ),
            out_shape=[jax.ShapeDtypeStruct((n * SPAN, query_width), jnp.bfloat16)]
            + parts[c * dp_size : (c + 1) * dp_size],
            in_specs=[vmem] * 2 + [anywhere] * len(halo_rows) + [vmem] * dp_size,
            out_specs=[vmem] * (1 + dp_size),
            scratch_shapes=scratch if ends else [],
            compiler_params=pltpu.CompilerParams(vmem_limit_bytes=16 * 1024 * 1024),
            name="attention",
        )(query, grad, *halo_rows, *kv[c])
        out_parts.append(out_rows)
        arrived = {0: kv_grads[0]}
        for s in order:
            arrived[s] = ring(kv_grads[s], -s)
        returned.append([arrived[s] for s in range(dp_size)])

    windows = jnp.concatenate(out_parts, 0)
    before = lax.ppermute(windows[row_count - SPAN :], "context", forth)
    position = lax.broadcasted_iota(jnp.int32, windows.shape, 0)
    cross_out = jnp.where(
        position % SPAN == SPAN - 1,
        windows,
        jnp.concatenate([before, windows[: row_count - SPAN]], 0),
    )
    collected = []
    for c in reversed(range(len(chunks))):
        collected = [
            pl.pallas_call(
                functools.partial(
                    collect_kernel,
                    owners=dp_size,
                    geometry=geometry,
                    first=sum(chunks[:c]) * KNB,
                    count=count,
                ),
                out_shape=jax.ShapeDtypeStruct(held.shape, jnp.bfloat16),
                in_specs=[smem] + [vmem] * dp_size + [anywhere] * len(collected),
                out_specs=anywhere,
                scratch_shapes=[pltpu.SemaphoreType.DMA((dp_size * chunks[c] * KNB,))],
                input_output_aliases={1 + dp_size: 0} if collected else {},
                compiler_params=params,
                name="collect",
            )(ids, *returned[c], *collected)
        ]
    final = lax.all_to_all(collected[0], group, 0, 0, tiled=True)
    final = final.reshape(tensor_size, dp_size, SLOTS, local_rows, rows, width)
    final = final.transpose(3, 1, 4, 2, 0, 5)
    return (cross_out[None], final.reshape(neighbour_kv.shape))


def solution(mesh):
    return jax.shard_map(
        shards,
        mesh=mesh,
        in_specs=(
            P("dp", "context", "tensor"),
            P("dp", "context", "tensor"),
            P(("dp", "context", "tensor"), None, None, None),
            P(),
        ),
        out_specs=(P("dp", "context", "tensor"), P(("dp", "context", "tensor"), None, None, None)),
        check_vma=False,
    )
```

```python
import functools
import math

import jax
import jax.numpy as jnp
from jax import lax
from jax.experimental import pallas as pl
from jax.experimental.pallas import tpu as pltpu
from jax.sharding import PartitionSpec as P

HD = 128
SPAN = 64
NL = 128
KNB = 2
SLOTS = 2
CHUNKS = (2, 2)
TAIL = 16
LOG2E = 1.4426950408889634


def nt(a, b):
    return lax.dot_general(a, b, (((1,), (1,)), ((), ())), preferred_element_type=jnp.float32)


def nn(a, b):
    return lax.dot_general(a, b, (((1,), (0,)), ((), ())), preferred_element_type=jnp.float32)


def split(value, size):
    if size & (size - 1) == 0:
        return lax.shift_right_logical(value, size.bit_length() - 1), value & (size - 1)
    return lax.div(value, size), lax.rem(value, size)


def place_of(row, geometry):
    local_rows, dp_size, context_size, tensor_size = geometry
    device, part = split(row, local_rows)
    tensor = split(device, tensor_size)[1]
    dp = split(device, context_size * tensor_size)[0]
    return tensor * dp_size + dp, part


def listed_places(ids_ref, blocks, spots, owners, geometry, count):
    me = ids_ref[owners * count]
    for block, (s, first) in zip(blocks, spots):
        start = split(me + s, owners)[1] * count + first
        for k in range(block.shape[0]):
            yield block, k, place_of(ids_ref[start + k], geometry)


def deliver_kernel(ids_ref, held_ref, *out_refs, **listing):
    for block, k, (source, part) in listed_places(ids_ref, out_refs, **listing):
        for slot in range(SLOTS):
            block[k, slot] = held_ref[source, slot, part]


def collect_kernel(ids_ref, *refs, spots, **listing):
    held_refs, (out_ref, sem) = refs[: len(spots)], refs[-2:]
    copies = [
        pltpu.make_async_copy(block.at[k], out_ref.at[source, :, part], sem.at[i])
        for i, (block, k, (source, part)) in enumerate(
            listed_places(ids_ref, held_refs, spots, **listing)
        )
    ]
    for copy in copies:
        copy.start()
    for copy in copies:
        copy.wait()


def attention_kernel(q_ref, g_ref, *refs, parts, halo, first):
    if halo:
        *sources, refs = refs[0], refs[1], refs[2:]
        *refs, halo_q_ref, halo_g_ref, sem = refs
        copies = [
            pltpu.make_async_copy(source, target, sem.at[i])
            for i, (source, target) in enumerate(zip(sources, (halo_q_ref, halo_g_ref)))
        ]
        for copy in copies:
            copy.start()
    kv_refs, out_ref, grad_refs = refs[:parts], refs[parts], refs[parts + 1 :]
    rows = kv_refs[0].shape[2]
    kv_heads = kv_refs[0].shape[3] // HD
    groups = out_ref.shape[1] // (kv_heads * HD)
    spans = out_ref.shape[0] // SPAN
    scale = 1.0 / math.sqrt(HD)
    swap = lax.broadcasted_iota(jnp.int32, (TAIL, HD), 0) == TAIL - 1

    def window(ref, halo_ref, span, lanes):
        end = (first + span + 1) * SPAN
        source, start = (halo_ref, 0) if halo and span == spans - 1 else (ref, end)
        stop = start + SPAN - TAIL
        tail = jnp.where(swap, ref[end - TAIL : end, lanes], source[stop : stop + TAIL, lanes])
        return [source[start:stop, lanes], tail]

    def load(span, h):
        places = [(p, span * KNB + n) for p in range(parts) for n in range(KNB)]
        lanes = slice(h * HD, (h + 1) * HD)
        heads = [slice((h * groups + g) * HD, (h * groups + g + 1) * HD) for g in range(groups)]
        key = jnp.concatenate([kv_refs[p][n, 0, :, lanes] for p, n in places], 0)
        value = jnp.concatenate([kv_refs[p][n, 1, :, lanes] for p, n in places], 0)
        halos = (halo_q_ref, halo_g_ref) if halo else (None, None)
        query, grad = (
            jnp.concatenate(sum([window(ref, halo_ref, span, s) for s in heads], []), 0)
            for ref, halo_ref in zip((q_ref, g_ref), halos)
        )
        return places, lanes, heads, key, value, query, grad

    stages = [range(spans - 1), range(spans - 1, spans)] if halo else [range(spans)]
    for stage in stages:
        if halo and spans - 1 in stage:
            for copy in copies:
                copy.wait()
        loaded = [(span,) + load(span, h) for span in stage for h in range(kv_heads)]
        all_scores = [nt(key, query) for *_, key, _, query, _ in loaded]
        slopes = [nt(value, grad) for *_, value, _, grad in loaded]
        all_raised = [
            jnp.exp2((scores - jnp.max(scores, axis=0, keepdims=True)) * (scale * LOG2E))
            for scores in all_scores
        ]
        shares = [1.0 / jnp.sum(raised, axis=0, keepdims=True) for raised in all_raised]
        for (span, places, lanes, heads, _, value, query, grad), raised, share, slope in zip(
            loaded, all_raised, shares, slopes
        ):
            low = (raised * share).astype(jnp.bfloat16)
            out = nn(value.T, low).T.astype(jnp.bfloat16)
            for g, s in enumerate(heads):
                out_ref[span * SPAN : (span + 1) * SPAN, s] = out[g * SPAN : (g + 1) * SPAN]
            value_grad = nn(low, grad).astype(jnp.bfloat16)
            centre = jnp.sum(raised * slope, axis=0, keepdims=True) * share
            score_grad = (raised * (share * scale) * (slope - centre)).astype(jnp.bfloat16)
            key_grad = nn(score_grad, query).astype(jnp.bfloat16)
            for b, (p, n) in enumerate(places):
                grad_refs[p][n, 0, :, lanes] = key_grad[b * rows : (b + 1) * rows]
                grad_refs[p][n, 1, :, lanes] = value_grad[b * rows : (b + 1) * rows]


def shards(cross_query, cross_grad, neighbour_kv, span_neighbours):
    dp_size = lax.axis_size("dp")
    context_size = lax.axis_size("context")
    tensor_size = lax.axis_size("tensor")
    local_rows, _, _, kv_width = neighbour_kv.shape
    width = kv_width // tensor_size
    row_count, query_width = cross_query.shape[1:]
    spans = row_count // SPAN
    count = spans * KNB
    peers = dp_size * tensor_size
    rows = NL // dp_size
    geometry = (local_rows, dp_size, context_size, tensor_size)
    group = ("tensor", "dp")
    params = pltpu.CompilerParams(vmem_limit_bytes=8 * 1024 * 1024)
    smem = pl.BlockSpec(memory_space=pltpu.SMEM)
    vmem = pl.BlockSpec(memory_space=pltpu.VMEM)

    def ring(array, by):
        return lax.ppermute(array, "dp", [(i, (i + by) % dp_size) for i in range(dp_size)])

    spread = neighbour_kv.transpose(2, 0, 1, 3)
    spread = spread.reshape(SLOTS, local_rows, dp_size, rows, tensor_size, width)
    spread = spread.transpose(4, 2, 0, 1, 3, 5).reshape(peers, SLOTS, local_rows, rows, width)
    ids = lax.dynamic_slice_in_dim(
        span_neighbours, lax.axis_index("context") * spans, spans, 1
    ).reshape(-1)
    ids = jnp.concatenate([ids, lax.axis_index("dp").astype(jnp.int32)[None]])
    query, grad = cross_query[0], cross_grad[0]
    spread, query, grad = lax.optimization_barrier((spread, query, grad))
    held = lax.all_to_all(spread, group, 0, 0, tiled=True)

    back = [(i + 1, i) for i in range(context_size - 1)]
    forth = [(i, i + 1) for i in range(context_size - 1)]
    halo = [lax.ppermute(values[:SPAN], "context", back) for values in (query, grad)]

    chunks = CHUNKS if sum(CHUNKS) == spans else (spans,)
    parts = [
        jax.ShapeDtypeStruct((n * KNB, SLOTS, rows, width), jnp.bfloat16)
        for n in chunks
        for _ in range(dp_size)
    ]
    listing = dict(owners=dp_size, geometry=geometry, count=count)
    spots = [
        [(s, sum(chunks[:c]) * KNB) for s in range(dp_size)] for c in range(len(chunks))
    ]
    delivered = pl.pallas_call(
        functools.partial(deliver_kernel, spots=sum(spots, []), **listing),
        out_shape=parts,
        in_specs=[smem, vmem],
        out_specs=[vmem] * len(parts),
        compiler_params=params,
        name="deliver",
    )(ids, held)
    order = sorted(range(1, dp_size), key=lambda s: -min(s, dp_size - s))
    kv = []
    for c in range(len(chunks)):
        mine = delivered[c * dp_size : (c + 1) * dp_size]
        arrived = {0: mine[0]}
        for s in order:
            arrived[s] = ring(mine[s], s)
        kv.append([arrived[s] for s in range(dp_size)])
    out_parts = []
    returned = []
    for c, n in enumerate(chunks):
        ends = c == len(chunks) - 1
        halo_rows = halo if ends else []
        anywhere = pl.BlockSpec(memory_space=pl.ANY)
        scratch = [pltpu.VMEM((SPAN, query_width), jnp.bfloat16)] * 2
        scratch.append(pltpu.SemaphoreType.DMA((2,)))
        out_rows, *kv_grads = pl.pallas_call(
            functools.partial(
                attention_kernel, parts=dp_size, halo=ends, first=sum(chunks[:c])
            ),
            out_shape=[jax.ShapeDtypeStruct((n * SPAN, query_width), jnp.bfloat16)]
            + parts[c * dp_size : (c + 1) * dp_size],
            in_specs=[vmem] * 2 + [anywhere] * len(halo_rows) + [vmem] * dp_size,
            out_specs=[vmem] * (1 + dp_size),
            scratch_shapes=scratch if ends else [],
            compiler_params=pltpu.CompilerParams(vmem_limit_bytes=16 * 1024 * 1024),
            name="attention",
        )(query, grad, *halo_rows, *kv[c])
        out_parts.append(out_rows)
        arrived = {0: kv_grads[0]}
        for s in order:
            arrived[s] = ring(kv_grads[s], -s)
        returned.append([arrived[s] for s in range(dp_size)])

    windows = jnp.concatenate(out_parts, 0)
    before = lax.ppermute(windows[row_count - SPAN :], "context", forth)
    position = lax.broadcasted_iota(jnp.int32, windows.shape, 0)
    cross_out = jnp.where(
        position % SPAN == SPAN - 1,
        windows,
        jnp.concatenate([before, windows[: row_count - SPAN]], 0),
    )
    half = dp_size // 2
    groups = [(c, range(dp_size)) for c in reversed(range(1, len(chunks)))]
    groups += [(0, range(half)), (0, range(half, dp_size))]
    collected = []
    for c, shifts in groups:
        arrays = [returned[c][s] for s in shifts]
        collected = [
            pl.pallas_call(
                functools.partial(
                    collect_kernel, spots=[spots[c][s] for s in shifts], **listing
                ),
                out_shape=jax.ShapeDtypeStruct(held.shape, jnp.bfloat16),
                in_specs=[smem] + [vmem] * len(arrays) + [anywhere] * len(collected),
                out_specs=anywhere,
                scratch_shapes=[pltpu.SemaphoreType.DMA((len(arrays) * chunks[c] * KNB,))],
                input_output_aliases={1 + len(arrays): 0} if collected else {},
                compiler_params=params,
                name="collect",
            )(ids, *arrays, *collected)
        ]
    final = lax.all_to_all(collected[0], group, 0, 0, tiled=True)
    final = final.reshape(tensor_size, dp_size, SLOTS, local_rows, rows, width)
    final = final.transpose(3, 1, 4, 2, 0, 5)
    return (cross_out[None], final.reshape(neighbour_kv.shape))


def solution(mesh):
    return jax.shard_map(
        shards,
        mesh=mesh,
        in_specs=(
            P("dp", "context", "tensor"),
            P("dp", "context", "tensor"),
            P(("dp", "context", "tensor"), None, None, None),
            P(),
        ),
        out_specs=(P("dp", "context", "tensor"), P(("dp", "context", "tensor"), None, None, None)),
        check_vma=False,
    )
```

```python
import functools
import math

import jax
import jax.numpy as jnp
from jax import lax
from jax.experimental import pallas as pl
from jax.experimental.pallas import tpu as pltpu
from jax.sharding import PartitionSpec as P

HD = 128
SPAN = 64
NL = 128
KNB = 2
SLOTS = 2
CHUNKS = (2, 2)
TAIL = 16
LOG2E = 1.4426950408889634


def nt(a, b):
    return lax.dot_general(a, b, (((1,), (1,)), ((), ())), preferred_element_type=jnp.float32)


def nn(a, b):
    return lax.dot_general(a, b, (((1,), (0,)), ((), ())), preferred_element_type=jnp.float32)


def split(value, size):
    if size & (size - 1) == 0:
        return lax.shift_right_logical(value, size.bit_length() - 1), value & (size - 1)
    return lax.div(value, size), lax.rem(value, size)


def place_of(row, geometry):
    local_rows, dp_size, context_size, tensor_size = geometry
    device, part = split(row, local_rows)
    tensor = split(device, tensor_size)[1]
    dp = split(device, context_size * tensor_size)[0]
    return tensor * dp_size + dp, part


def listed_places(ids_ref, blocks, spots, owners, geometry, count):
    me = ids_ref[owners * count]
    for block, (s, first) in zip(blocks, spots):
        start = split(me + s, owners)[1] * count + first
        for k in range(block.shape[0]):
            yield block, k, place_of(ids_ref[start + k], geometry)


def deliver_kernel(ids_ref, held_ref, *out_refs, **listing):
    for block, k, (source, part) in listed_places(ids_ref, out_refs, **listing):
        for slot in range(SLOTS):
            block[k, slot] = held_ref[source, part, slot]


def collect_kernel(ids_ref, *refs, spots, **listing):
    held_refs, (out_ref, sem) = refs[: len(spots)], refs[-2:]
    copies = [
        pltpu.make_async_copy(block.at[k], out_ref.at[source, part], sem.at[i])
        for i, (block, k, (source, part)) in enumerate(
            listed_places(ids_ref, held_refs, spots, **listing)
        )
    ]
    for copy in copies:
        copy.start()
    for copy in copies:
        copy.wait()


def attention_kernel(q_ref, g_ref, *refs, parts, halo, first):
    if halo:
        *sources, refs = refs[0], refs[1], refs[2:]
        *refs, halo_q_ref, halo_g_ref, sem = refs
        copies = [
            pltpu.make_async_copy(source, target, sem.at[i])
            for i, (source, target) in enumerate(zip(sources, (halo_q_ref, halo_g_ref)))
        ]
        for copy in copies:
            copy.start()
    kv_refs, out_ref, grad_refs = refs[:parts], refs[parts], refs[parts + 1 :]
    rows = kv_refs[0].shape[2]
    kv_heads = kv_refs[0].shape[3] // HD
    groups = out_ref.shape[1] // (kv_heads * HD)
    spans = out_ref.shape[0] // SPAN
    scale = 1.0 / math.sqrt(HD)
    swap = lax.broadcasted_iota(jnp.int32, (TAIL, HD), 0) == TAIL - 1

    def window(ref, halo_ref, span, lanes):
        end = (first + span + 1) * SPAN
        source, start = (halo_ref, 0) if halo and span == spans - 1 else (ref, end)
        stop = start + SPAN - TAIL
        tail = jnp.where(swap, ref[end - TAIL : end, lanes], source[stop : stop + TAIL, lanes])
        return [source[start:stop, lanes], tail]

    def load(span, h):
        places = [(p, span * KNB + n) for p in range(parts) for n in range(KNB)]
        lanes = slice(h * HD, (h + 1) * HD)
        heads = [slice((h * groups + g) * HD, (h * groups + g + 1) * HD) for g in range(groups)]
        key = jnp.concatenate([kv_refs[p][n, 0, :, lanes] for p, n in places], 0)
        value = jnp.concatenate([kv_refs[p][n, 1, :, lanes] for p, n in places], 0)
        halos = (halo_q_ref, halo_g_ref) if halo else (None, None)
        query, grad = (
            jnp.concatenate(sum([window(ref, halo_ref, span, s) for s in heads], []), 0)
            for ref, halo_ref in zip((q_ref, g_ref), halos)
        )
        return places, lanes, heads, key, value, query, grad

    stages = [range(spans - 1), range(spans - 1, spans)] if halo else [range(spans)]
    for stage in stages:
        if halo and spans - 1 in stage:
            for copy in copies:
                copy.wait()
        loaded = [(span,) + load(span, h) for span in stage for h in range(kv_heads)]
        all_scores = [nt(key, query) for *_, key, _, query, _ in loaded]
        slopes = [nt(value, grad) for *_, value, _, grad in loaded]
        all_raised = [
            jnp.exp2((scores - jnp.max(scores, axis=0, keepdims=True)) * (scale * LOG2E))
            for scores in all_scores
        ]
        shares = [1.0 / jnp.sum(raised, axis=0, keepdims=True) for raised in all_raised]
        for (span, places, lanes, heads, _, value, query, grad), raised, share, slope in zip(
            loaded, all_raised, shares, slopes
        ):
            low = (raised * share).astype(jnp.bfloat16)
            out = nn(value.T, low).T.astype(jnp.bfloat16)
            for g, s in enumerate(heads):
                out_ref[span * SPAN : (span + 1) * SPAN, s] = out[g * SPAN : (g + 1) * SPAN]
            value_grad = nn(low, grad).astype(jnp.bfloat16)
            centre = jnp.sum(raised * slope, axis=0, keepdims=True) * share
            score_grad = (raised * (share * scale) * (slope - centre)).astype(jnp.bfloat16)
            key_grad = nn(score_grad, query).astype(jnp.bfloat16)
            for b, (p, n) in enumerate(places):
                grad_refs[p][n, 0, :, lanes] = key_grad[b * rows : (b + 1) * rows]
                grad_refs[p][n, 1, :, lanes] = value_grad[b * rows : (b + 1) * rows]


def shards(cross_query, cross_grad, neighbour_kv, span_neighbours):
    dp_size = lax.axis_size("dp")
    context_size = lax.axis_size("context")
    tensor_size = lax.axis_size("tensor")
    local_rows, _, _, kv_width = neighbour_kv.shape
    width = kv_width // tensor_size
    row_count, query_width = cross_query.shape[1:]
    spans = row_count // SPAN
    count = spans * KNB
    peers = dp_size * tensor_size
    rows = NL // dp_size
    geometry = (local_rows, dp_size, context_size, tensor_size)
    group = ("tensor", "dp")
    params = pltpu.CompilerParams(vmem_limit_bytes=8 * 1024 * 1024)
    smem = pl.BlockSpec(memory_space=pltpu.SMEM)
    vmem = pl.BlockSpec(memory_space=pltpu.VMEM)

    def ring(array, by):
        return lax.ppermute(array, "dp", [(i, (i + by) % dp_size) for i in range(dp_size)])

    spread = neighbour_kv.transpose(2, 0, 1, 3)
    spread = spread.reshape(SLOTS, local_rows, dp_size, rows, tensor_size, width)
    spread = spread.transpose(4, 2, 1, 0, 3, 5).reshape(peers, local_rows, SLOTS, rows, width)
    ids = lax.dynamic_slice_in_dim(
        span_neighbours, lax.axis_index("context") * spans, spans, 1
    ).reshape(-1)
    ids = jnp.concatenate([ids, lax.axis_index("dp").astype(jnp.int32)[None]])
    query, grad = cross_query[0], cross_grad[0]
    spread, query, grad = lax.optimization_barrier((spread, query, grad))
    held = lax.all_to_all(spread, group, 0, 0, tiled=True)

    back = [(i + 1, i) for i in range(context_size - 1)]
    forth = [(i, i + 1) for i in range(context_size - 1)]
    halo = [lax.ppermute(values[:SPAN], "context", back) for values in (query, grad)]

    chunks = CHUNKS if sum(CHUNKS) == spans else (spans,)
    parts = [
        jax.ShapeDtypeStruct((n * KNB, SLOTS, rows, width), jnp.bfloat16)
        for n in chunks
        for _ in range(dp_size)
    ]
    listing = dict(owners=dp_size, geometry=geometry, count=count)
    spots = [
        [(s, sum(chunks[:c]) * KNB) for s in range(dp_size)] for c in range(len(chunks))
    ]
    delivered = pl.pallas_call(
        functools.partial(deliver_kernel, spots=sum(spots, []), **listing),
        out_shape=parts,
        in_specs=[smem, vmem],
        out_specs=[vmem] * len(parts),
        compiler_params=params,
        name="deliver",
    )(ids, held)
    order = sorted(range(1, dp_size), key=lambda s: -min(s, dp_size - s))
    kv = []
    for c in range(len(chunks)):
        mine = delivered[c * dp_size : (c + 1) * dp_size]
        arrived = {0: mine[0]}
        for s in order:
            arrived[s] = ring(mine[s], s)
        kv.append([arrived[s] for s in range(dp_size)])
    out_parts = []
    returned = []
    for c, n in enumerate(chunks):
        ends = c == len(chunks) - 1
        halo_rows = halo if ends else []
        anywhere = pl.BlockSpec(memory_space=pl.ANY)
        scratch = [pltpu.VMEM((SPAN, query_width), jnp.bfloat16)] * 2
        scratch.append(pltpu.SemaphoreType.DMA((2,)))
        out_rows, *kv_grads = pl.pallas_call(
            functools.partial(
                attention_kernel, parts=dp_size, halo=ends, first=sum(chunks[:c])
            ),
            out_shape=[jax.ShapeDtypeStruct((n * SPAN, query_width), jnp.bfloat16)]
            + parts[c * dp_size : (c + 1) * dp_size],
            in_specs=[vmem] * 2 + [anywhere] * len(halo_rows) + [vmem] * dp_size,
            out_specs=[vmem] * (1 + dp_size),
            scratch_shapes=scratch if ends else [],
            compiler_params=pltpu.CompilerParams(vmem_limit_bytes=16 * 1024 * 1024),
            name="attention",
        )(query, grad, *halo_rows, *kv[c])
        out_parts.append(out_rows)
        arrived = {0: kv_grads[0]}
        for s in order:
            arrived[s] = ring(kv_grads[s], -s)
        returned.append([arrived[s] for s in range(dp_size)])

    windows = jnp.concatenate(out_parts, 0)
    before = lax.ppermute(windows[row_count - SPAN :], "context", forth)
    position = lax.broadcasted_iota(jnp.int32, windows.shape, 0)
    cross_out = jnp.where(
        position % SPAN == SPAN - 1,
        windows,
        jnp.concatenate([before, windows[: row_count - SPAN]], 0),
    )
    half = dp_size // 2
    groups = [(c, range(dp_size)) for c in reversed(range(1, len(chunks)))]
    groups += [(0, range(half)), (0, range(half, dp_size))]
    collected = []
    for c, shifts in groups:
        arrays = [returned[c][s] for s in shifts]
        collected = [
            pl.pallas_call(
                functools.partial(
                    collect_kernel, spots=[spots[c][s] for s in shifts], **listing
                ),
                out_shape=jax.ShapeDtypeStruct(held.shape, jnp.bfloat16),
                in_specs=[smem] + [vmem] * len(arrays) + [anywhere] * len(collected),
                out_specs=anywhere,
                scratch_shapes=[pltpu.SemaphoreType.DMA((len(arrays) * chunks[c] * KNB,))],
                input_output_aliases={1 + len(arrays): 0} if collected else {},
                compiler_params=params,
                name="collect",
            )(ids, *arrays, *collected)
        ]
    final = lax.all_to_all(collected[0], group, 0, 0, tiled=True)
    final = final.reshape(tensor_size, dp_size, local_rows, SLOTS, rows, width)
    final = final.transpose(2, 1, 4, 3, 0, 5)
    return (cross_out[None], final.reshape(neighbour_kv.shape))


def solution(mesh):
    return jax.shard_map(
        shards,
        mesh=mesh,
        in_specs=(
            P("dp", "context", "tensor"),
            P("dp", "context", "tensor"),
            P(("dp", "context", "tensor"), None, None, None),
            P(),
        ),
        out_specs=(P("dp", "context", "tensor"), P(("dp", "context", "tensor"), None, None, None)),
        check_vma=False,
    )
```
